256 devices in a mesh: byte: 32 (over y, x, core), tensor: 8 (over z).
Axes of the slice: x: 4, y: 4, z: 8, core: 2. Of those that a mesh axis runs over, the one named last changes fastest.
Arguments:
- byte_states: bfloat16 [65536, 1280], P(('byte', 'tensor')), may hold values from -6 to 6
- enc_gain: float32 [1280], replicated, may hold values from 0.1 to 1.9
- patch_lengths: int32 [256, 32], P(('byte', 'tensor')), may hold values from 1 to 16, 256 in all within a row
- patch_route: int32 [256, 32, 1], P(('byte', 'tensor')), may hold values from 0 to 31; in each aligned block of 32 rows (0 to 31, 32 to 63, ..., all dimensions but the last counted through in order) at most 2 rows name the same one
- w_in: bfloat16 [1280, 4096], P(None, 'tensor'), may hold values from -0.15625 to 0.15625
- latent_gain: float32 [4096], replicated, may hold values from 0.1 to 1.9
- w_query: bfloat16 [4096, 4096], P('byte', 'tensor'), may hold values from -1 to 1
- w_key: bfloat16 [4096, 4096], P('byte', 'tensor'), may hold values from -24 to 24
- w_value: bfloat16 [4096, 4096], P('byte', 'tensor'), may hold values from -0.09375 to 0.09375
- w_attn_out: bfloat16 [4096, 4096], P('tensor', 'byte'), may hold values from -0.09375 to 0.09375
- w_out: bfloat16 [4096, 1280], P('tensor'), may hold values from -0.09375 to 0.09375
- w_head: bfloat16 [1280, 256], replicated, may hold values from -0.15625 to 0.15625
Outputs:
- logits: bfloat16 [65536, 256], P(('byte', 'tensor'))
The draws below stay inside these ranges and needn't reach their ends.
Inputs may be any that keep to these rules, and one draw needn't show every extreme that they name: `patch_lengths`: each device's lengths sum to 256; some patch has exactly 16 bytes. `patch_route`: at most 2 patches of one device name the same latent index, and that many are reached.
All inputs are finite; a program needn't handle non-finite values.
Results may differ from the reference program's by a relative error of at most 0.02.
Values may be sent and summed in bfloat16 or wider, within the bound.
A program may use at most 128 MiB of HBM per device.

```python
import math
import jax
import jax.numpy as jnp
import numpy as np
from jax import lax

D = 4096
E = 1280
DH = 128
VOCAB = 256
BDEV = 256
MAXLEN = 16
PDEV = 32
CAP = 2
CTX = 512
HW = 4096
BYTES = 65536
N_BYTE = 32
N_TENSOR = 8
DEVICES = 256


def shared_query(key):
    return jnp.clip(jax.random.normal(key, (D, HW), jnp.float32), -4.0, 4.0) * D ** (-0.5)


def draw_w_query(key, part):
    return shared_query(key).astype(jnp.bfloat16)


def draw_w_key(key, part):
    key = jax.random.fold_in(key, 7)
    return (jnp.clip(jax.random.normal(key, (D, HW), jnp.float32), -4.0, 4.0) * D ** (-0.5)).astype(jnp.bfloat16)


def block_levels(stream_key, shape, cuts, smallest, high):
    loudness = 1.0
    for dim, shards_of in cuts:
        steps = jax.random.uniform(jax.random.fold_in(jax.random.fold_in(stream_key, 6), dim), (shards_of,), jnp.float32, smallest / len(cuts), high / len(cuts))
        loudness = loudness * jnp.repeat(jnp.exp(steps), shape[dim] // shards_of).reshape((-1,) + (1,) * (len(shape) - 1 - dim))
    return loudness


def profile(number_of, total, most, lean):
    weights = [(1 << 20) // math.isqrt(grade ** lean) + 1 for grade in range(2, number_of + 1)]
    surplus, given = total - most - (number_of - 1), [1] * (number_of - 1)
    while surplus > 0:
        free = [i for i in range(number_of - 1) if given[i] < most]
        pool, budget = sum([weights[i] for i in free]), surplus
        for i in free:
            more = min(most - given[i], max(1, budget * weights[i] // pool), surplus)
            given[i] = given[i] + more
            surplus = surplus - more
    return np.array([most] + given)


def ragged(own_key, count, total, most, skew):
    if count == 2:
        one = jax.random.randint(own_key, (), max(1, total - most), min(most, total - 1) + 1)
        return jnp.stack([one, total - one])
    tallies = jnp.asarray(profile(count, total, most, skew), jnp.int32)
    twos = (count - 1) // 2
    donor, taker = tallies[1:1 + 2 * twos:2], tallies[2:2 + 2 * twos:2]
    margin = jnp.minimum(donor - 1, most - taker)
    shifted = jax.random.randint(jax.random.fold_in(own_key, 1), (twos,), 0, 1 << 20) % (margin + 1)
    tallies = tallies.at[1:1 + 2 * twos:2].set(donor - shifted).at[2:2 + 2 * twos:2].set(taker + shifted)
    return tallies[jax.random.permutation(jax.random.fold_in(own_key, 2), count)]


def shared_out(rng, own, number, rows, amount, top, reach, skew):
    sequence = jax.random.permutation(rng, amount)
    heavy_load, common = shares(amount, rows * top, reach, skew, True), shares(amount, rows * top, reach, skew, False)
    places = jnp.arange(amount)

    def named(tallies, turn):
        used = int((tallies > 0).sum())
        fixed = max(1, used // 4)
        moved = fixed + (places - fixed + turn * (used - fixed)) % max(1, amount - fixed)
        return jnp.zeros((amount,), jnp.int32).at[sequence[jnp.where(places < fixed, places, moved)]].set(jnp.asarray(tallies, jnp.int32))

    tallies = jnp.where(number % 4 == 0, named(heavy_load, number // 4), named(common, number - number // 4 - 1))
    mixed = jax.random.permutation(jax.random.fold_in(own, 3), amount)
    source_of, taker = mixed[0:amount // 2 * 2:2], mixed[1:amount // 2 * 2:2]
    slack = jnp.minimum(tallies[source_of] - 1, reach - tallies[taker]) // 2
    slack = jnp.where((source_of == sequence[0]) | (taker == sequence[0]) | (tallies[taker] == 0), 0, jnp.maximum(slack, 0))
    moved = jax.random.randint(jax.random.fold_in(own, 4), (amount // 2,), 0, 1 << 20) % (slack + 1)
    tallies = tallies.at[source_of].add(-moved).at[taker].add(moved)
    labels = jnp.searchsorted(jnp.cumsum(tallies), jnp.arange(rows * top), side="right").astype(jnp.int32)
    listing = labels.reshape(top, rows).T
    listing = listing[jax.random.permutation(jax.random.fold_in(own, 1), rows)]
    turn = jax.random.randint(jax.random.fold_in(own, 2), (rows, 1), 0, top)
    return jnp.take_along_axis(listing, (jnp.arange(top)[None, :] + turn) % top, axis=1)


def shares(count, total, reach, slope, full):
    weights = [(1 << 20) // math.isqrt(standing ** slope) + 1 for standing in range(1, count + 1)]
    largest = reach if full else min(reach, max(-(-total // count), total * weights[0] // sum(weights)))
    least = 1 if total - largest >= count - 1 else 0
    holding, spare = [largest] + [least] * (count - 1), total - largest - least * (count - 1)
    while spare > 0:
        candidates = [i for i in range(1, count) if holding[i] < largest] or [i for i in range(1, count) if holding[i] < reach]
        whole, left = sum([weights[i] for i in candidates]), spare
        for i in candidates:
            more = min(reach - holding[i], max(1, left * weights[i] // whole), spare)
            holding[i] = holding[i] + more
            spare = spare - more
    return np.array(holding)


def centred(rng, extent, deviation, reach, shards=(), kind=jnp.bfloat16):
    drawn = deviation * jax.random.normal(rng, extent, jnp.float32)
    if shards:
        drawn = drawn * block_levels(rng, extent, shards, -0.22, 0.18)
    return jnp.clip(drawn, -reach, reach).astype(kind)


def setup_inputs(seed: int = 0) -> dict:
    splits = jax.random.split(jax.random.key(seed), 13)
    byte_states = centred(splits[0], (BYTES, E), 1.0, 6.0, ((0, 256),))
    enc_gain = jnp.clip(1.0 + 0.18 * jax.random.normal(splits[1], (E,), jnp.float32), 0.1, 1.9)
    patch_lengths = jax.vmap(lambda own: ragged(own, PDEV, BDEV, MAXLEN, 2))(jax.random.split(splits[2], DEVICES)).reshape((DEVICES, PDEV)).astype(jnp.int32)
    patch_route_keys = jax.random.split(jax.random.fold_in(splits[3], 1), DEVICES * PDEV // PDEV)
    patch_route_turns = jax.random.permutation(jax.random.fold_in(splits[3], 3), DEVICES * PDEV // PDEV)
    patch_route = jax.vmap(lambda own, number: shared_out(jax.random.fold_in(splits[3], 2), own, number, PDEV, N_BYTE, 1, CAP, 2))(patch_route_keys, patch_route_turns).reshape((DEVICES, PDEV, 1))
    w_in = centred(splits[4], (E, D), E ** -0.5, 0.15625, ((1, 8),))
    latent_gain = jnp.clip(1.0 + 0.18 * jax.random.normal(splits[5], (D,), jnp.float32), 0.1, 1.9)
    w_query = draw_w_query(jax.random.fold_in(splits[12], 71), 0)
    w_key = draw_w_key(jax.random.fold_in(splits[12], 71), 0)
    w_value = centred(splits[8], (D, HW), D ** -0.5, 0.09375, ((0, 32), (1, 8)))
    w_attn_out = centred(splits[9], (HW, D), HW ** -0.5, 0.09375, ((0, 8), (1, 32)))
    w_out = centred(splits[10], (D, E), D ** -0.5, 0.09375, ((0, 8),))
    w_head = centred(splits[11], (E, VOCAB), E ** -0.5, 0.15625)
    return dict(byte_states=byte_states, enc_gain=enc_gain, patch_lengths=patch_lengths, patch_route=patch_route, w_in=w_in, latent_gain=latent_gain, w_query=w_query, w_key=w_key, w_value=w_value, w_attn_out=w_attn_out, w_out=w_out, w_head=w_head)


EPS = 1e-06

def rms_scale(values, scaling):
    values = values.astype(jnp.float32)
    return values * lax.rsqrt(lax.optimization_barrier(jnp.mean(values * values, axis=-1, keepdims=True)) + EPS) * scaling.astype(jnp.float32)

def patch_tables(lengths, routing, n_dest, capacity, n_bytes):
    lengths = lengths.astype(jnp.int32)
    ending = jnp.cumsum(lengths).astype(jnp.int32)
    starting = ending - lengths
    places = jnp.arange(n_bytes, dtype=jnp.int32)
    member = ((places[None, :] >= starting[:, None]) & (places[None, :] < ending[:, None])).astype(jnp.float32)
    onehot = (routing[:, None] == jnp.arange(n_dest, dtype=jnp.int32)[None, :]).astype(jnp.int32)
    earlier = (jnp.cumsum(onehot, axis=0) - onehot).astype(jnp.int32)
    slots = lax.optimization_barrier(jnp.sum(earlier * onehot, axis=1)).astype(jnp.int32)
    target = routing * capacity + slots
    select = (target[None, :] == jnp.arange(n_dest * capacity, dtype=jnp.int32)[:, None]).astype(jnp.float32)
    return (member, select)

def pool_bytes(states, scaling, lengths, member):
    normed = rms_scale(states, scaling)
    summed = jnp.dot(member, normed, precision=lax.Precision.HIGHEST, preferred_element_type=jnp.float32)
    return (summed / lengths[:, None].astype(jnp.float32)).astype(jnp.bfloat16)

def attend(queries, key_rows, value_rows, visible_slots, head_size):
    length = queries.shape[0]
    n_heads = queries.shape[1] // head_size
    query_heads = queries.reshape(length, n_heads, head_size).astype(jnp.float32)
    key_heads = key_rows.reshape(length, n_heads, head_size).astype(jnp.float32)
    value_heads = value_rows.reshape(length, n_heads, head_size).astype(jnp.float32)
    scores = jnp.einsum('qhd,khd->hqk', query_heads, key_heads) * head_size ** (-0.5)
    places = jnp.arange(length, dtype=jnp.int32)
    allowed = (places[None, :] < places[:, None]) & (visible_slots[None, :] > 0) | (places[None, :] == places[:, None])
    scores = jnp.where(allowed[None, :, :], scores, -1e+30)
    highest = lax.optimization_barrier(jnp.max(scores, axis=-1, keepdims=True))
    raised = jnp.exp(scores - highest)
    weights = (raised / lax.optimization_barrier(jnp.sum(raised, axis=-1, keepdims=True))).astype(jnp.bfloat16)
    mixed = jnp.einsum('hqk,khd->qhd', weights.astype(jnp.float32), value_heads)
    return mixed.astype(jnp.bfloat16).reshape(length, n_heads * head_size)

def reference(byte_states, enc_gain, patch_lengths, patch_route, w_in, latent_gain, w_query, w_key, w_value, w_attn_out, w_out, w_head):
    devices = N_BYTE * N_TENSOR
    states = byte_states.reshape(devices, BDEV, E)

    def encode(items):
        rows_here, lengths, routing = items
        member, select = patch_tables(lengths, routing[:, 0], N_BYTE, CAP, BDEV)
        pooled = pool_bytes(rows_here, enc_gain, lengths, member)
        sending = jnp.dot(select.astype(jnp.bfloat16), pooled, preferred_element_type=jnp.float32).astype(jnp.bfloat16)
        used = lax.optimization_barrier(jnp.sum(select, axis=1)).astype(jnp.int32)
        return (sending, used)
    sendings, useds = lax.map(encode, (states, patch_lengths, patch_route))
    context = sendings.reshape(N_BYTE, N_TENSOR, N_BYTE, CAP, E).transpose(2, 1, 0, 3, 4).reshape(N_BYTE, CTX, E)
    visible = useds.reshape(N_BYTE, N_TENSOR, N_BYTE, CAP).transpose(2, 1, 0, 3).reshape(N_BYTE, CTX)

    def latent_step(items):
        slots, slot_used = items
        latent = jnp.dot(slots, w_in, preferred_element_type=jnp.float32).astype(jnp.bfloat16)
        normed = rms_scale(latent, latent_gain).astype(jnp.bfloat16)
        queries = jnp.dot(normed, w_query, preferred_element_type=jnp.float32).astype(jnp.bfloat16)
        key_rows = jnp.dot(normed, w_key, preferred_element_type=jnp.float32).astype(jnp.bfloat16)
        value_rows = jnp.dot(normed, w_value, preferred_element_type=jnp.float32).astype(jnp.bfloat16)
        attended = attend(queries, key_rows, value_rows, slot_used, DH)
        projected = jnp.dot(attended, w_attn_out, preferred_element_type=jnp.float32)
        updated = (latent.astype(jnp.float32) + projected).astype(jnp.bfloat16)
        return jnp.dot(updated, w_out, preferred_element_type=jnp.float32).astype(jnp.bfloat16)
    results = lax.map(latent_step, (context, visible))
    returned = results.reshape(N_BYTE, N_TENSOR, N_BYTE, CAP, E).transpose(2, 1, 0, 3, 4).reshape(devices, N_BYTE * CAP, E)

    def decode(items):
        rows_here, lengths, routing, arrived = items
        member, select = patch_tables(lengths, routing[:, 0], N_BYTE, CAP, BDEV)
        patch_values = jnp.dot(select.T.astype(jnp.bfloat16), arrived, preferred_element_type=jnp.float32)
        spread = jnp.dot(member.T, patch_values, precision=lax.Precision.HIGHEST, preferred_element_type=jnp.float32)
        decoded = (rows_here.astype(jnp.float32) + spread).astype(jnp.bfloat16)
        return jnp.dot(decoded, w_head, preferred_element_type=jnp.float32).astype(jnp.bfloat16)
    outputs = lax.map(decode, (states, patch_lengths, patch_route, returned))
    return outputs.reshape(devices * BDEV, VOCAB)
```

```python
import jax
import jax.numpy as jnp
from jax import lax
from jax.sharding import PartitionSpec as P

DH = 128


EPS = 1e-06


def rms_scale(values, scaling):
    values = values.astype(jnp.float32)
    return values * lax.rsqrt(jnp.mean(values * values, axis=-1, keepdims=True) + EPS) * scaling


def patch_tables(lengths, routing, n_dest, capacity, n_bytes):
    ending = jnp.cumsum(lengths)
    starting = ending - lengths
    places = jnp.arange(n_bytes, dtype=jnp.int32)
    member = ((places[None, :] >= starting[:, None]) & (places[None, :] < ending[:, None])).astype(
        jnp.float32
    )
    onehot = (routing[:, None] == jnp.arange(n_dest, dtype=jnp.int32)[None, :]).astype(jnp.int32)
    earlier = jnp.cumsum(onehot, axis=0) - onehot
    slots = jnp.sum(earlier * onehot, axis=1)
    target = routing * capacity + slots
    select = (target[None, :] == jnp.arange(n_dest * capacity, dtype=jnp.int32)[:, None]).astype(
        jnp.float32
    )
    return (member, select)


def attend(queries, key_rows, value_rows, visible_slots, head_size):
    length = queries.shape[0]
    n_heads = queries.shape[1] // head_size
    query_heads = queries.reshape(length, n_heads, head_size)
    key_heads = key_rows.reshape(length, n_heads, head_size)
    value_heads = value_rows.reshape(length, n_heads, head_size)
    scores = jnp.einsum(
        "qhd,khd->hqk", query_heads, key_heads, preferred_element_type=jnp.float32
    ) * head_size ** (-0.5)
    places = jnp.arange(length, dtype=jnp.int32)
    allowed = (places[None, :] < places[:, None]) & (visible_slots[None, :] > 0) | (
        places[None, :] == places[:, None]
    )
    scores = jnp.where(allowed[None, :, :], scores, -1e30)
    highest = jnp.max(scores, axis=-1, keepdims=True)
    raised = jnp.exp(scores - highest)
    weights = (raised / jnp.sum(raised, axis=-1, keepdims=True)).astype(jnp.bfloat16)
    mixed = jnp.einsum("hqk,khd->qhd", weights, value_heads, preferred_element_type=jnp.float32)
    return mixed.astype(jnp.bfloat16).reshape(length, n_heads * head_size)


def dot(a, b):
    return jnp.dot(a, b, preferred_element_type=jnp.float32)


def body(
    byte_states,
    enc_gain,
    patch_lengths,
    patch_route,
    w_in,
    latent_gain,
    w_query,
    w_key,
    w_value,
    w_attn_out,
    w_out,
    w_head,
):
    byte_count = lax.axis_size("byte")
    byte_place = lax.axis_index("byte")
    tensor_place = lax.axis_index("tensor")
    byte_rows, byte_width = byte_states.shape
    depth = w_query.shape[0]
    columns = w_in.shape[1]
    per = columns // depth

    holder = tensor_place == byte_place // per
    offset = (byte_place % per) * depth
    sub_in = lax.dynamic_slice_in_dim(w_in, offset, depth, 1)
    sub_out = lax.dynamic_slice_in_dim(w_out, offset, depth, 0)
    both = jnp.concatenate([sub_in.T, sub_out], axis=0)
    both = lax.psum(jnp.where(holder, both, jnp.zeros_like(both)), "tensor")
    gain = lax.dynamic_slice_in_dim(latent_gain, byte_place * depth, depth, 0)
    sub_in = (both[:depth].astype(jnp.float32) * gain[:, None]).astype(jnp.bfloat16)
    sub_out = both[depth:]
    parts = [
        lax.dot_general(
            left, weight, (((0,), (0,)), ((), ())), preferred_element_type=jnp.float32
        ).astype(jnp.bfloat16)
        for left, weight in (
            (sub_in, w_query),
            (sub_in, w_key),
            (sub_in, w_value),
            (sub_out, w_attn_out.T),
        )
    ]
    partial = jnp.concatenate(parts, axis=0)
    shares = lax.psum_scatter(partial, "byte", scatter_dimension=0, tiled=True)
    fused = lax.all_gather(shares, "byte", axis=0, tiled=True)
    m_query, m_key, m_value, m_out = jnp.split(fused, 4, axis=0)

    lengths = patch_lengths[0]
    routing = patch_route[0, :, 0]
    patch_count = lengths.shape[0]
    capacity = max(2, 2 * patch_count // byte_count)
    member, select = patch_tables(lengths, routing, byte_count, capacity, byte_rows)
    normed_bytes = rms_scale(byte_states, enc_gain)
    summed = jnp.dot(
        member, normed_bytes, precision=lax.Precision.HIGHEST, preferred_element_type=jnp.float32
    )
    pooled = (summed / lengths[:, None].astype(jnp.float32)).astype(jnp.bfloat16)
    sending = dot(select.astype(jnp.bfloat16), pooled).astype(jnp.bfloat16)
    used_slots = jnp.sum(select, axis=1).astype(jnp.bfloat16)
    sending = jnp.concatenate(
        [sending, jnp.broadcast_to(used_slots[:, None], (sending.shape[0], 128))], axis=1
    )
    width = byte_width + 128
    arrived = lax.all_to_all(
        sending.reshape(byte_count, capacity, width),
        "byte",
        split_axis=0,
        concat_axis=0,
        tiled=True,
    )
    own_rows = byte_count * capacity
    context = lax.all_gather(arrived.reshape(own_rows, width), "tensor", axis=0, tiled=True)
    context_used = context[:, byte_width]
    context = context[:, :byte_width]
    latent_part = dot(context, w_in).astype(jnp.bfloat16)
    squares = jnp.sum(jnp.square(latent_part.astype(jnp.float32)), axis=-1)
    squares = lax.psum(squares, "tensor")
    scale = lax.rsqrt(squares / latent_gain.shape[0] + EPS)[:, None]
    attended = attend(
        (dot(context, m_query) * scale).astype(jnp.bfloat16),
        (dot(context, m_key) * scale).astype(jnp.bfloat16),
        (dot(context, m_value) * scale).astype(jnp.bfloat16),
        context_used,
        DH,
    )
    partial_value = dot(latent_part, w_out) + lax.dot_general(
        attended, m_out, (((1,), (1,)), ((), ())), preferred_element_type=jnp.float32
    )
    outgoing = lax.psum_scatter(
        partial_value.astype(jnp.bfloat16), "tensor", scatter_dimension=0, tiled=True
    )
    returned = lax.all_to_all(
        outgoing.reshape(byte_count, capacity, byte_width),
        "byte",
        split_axis=0,
        concat_axis=0,
        tiled=True,
    )
    patch_values = dot(select.T.astype(jnp.bfloat16), returned.reshape(own_rows, byte_width))
    spread = jnp.dot(
        member.T, patch_values, precision=lax.Precision.HIGHEST, preferred_element_type=jnp.float32
    )
    decoded = (byte_states.astype(jnp.float32) + spread).astype(jnp.bfloat16)
    return dot(decoded, w_head).astype(jnp.bfloat16)


def solution(mesh):
    return jax.shard_map(
        body,
        mesh=mesh,
        in_specs=(
            P(("byte", "tensor"), None),
            P(),
            P(("byte", "tensor"), None),
            P(("byte", "tensor"), None, None),
            P(None, "tensor"),
            P(),
            P("byte", "tensor"),
            P("byte", "tensor"),
            P("byte", "tensor"),
            P("tensor", "byte"),
            P("tensor", None),
            P(),
        ),
        out_specs=P(("byte", "tensor"), None),
        check_vma=False,
    )
```

```python
import jax
import jax.numpy as jnp
from jax import lax
from jax.experimental import pallas as pl
from jax.experimental.pallas import tpu as pltpu
from jax.sharding import PartitionSpec as P

MESH = pl.DeviceIdType.MESH
BF16 = jnp.bfloat16
F32 = jnp.float32
DH = 128
EPS = 1e-06
SIDE = 4
NB = 32
NT = 8
E = 1280
D = 4096
CTX = 512
W = 256
PIECES = E // W
STAGES = 2 * PIECES
FLAGS = 128
PACK = 16


def mm(a, b):
    return jnp.dot(a, b, preferred_element_type=F32)


def mm_t(a, b):
    return lax.dot_general(a, b, (((1,), (1,)), ((), ())), preferred_element_type=F32)


def iota(shape, dim):
    return lax.broadcasted_iota(jnp.int32, shape, dim)


def onehot(mask):
    return jnp.where(mask, 1.0, 0.0).astype(BF16)


def tables(lengths, route):
    n = lengths.shape[1]
    down, across = iota((n, n), 0), iota((n, n), 1)
    eye = down == across

    def column(row):
        return jnp.sum(jnp.where(eye, row, 0.0), axis=1, keepdims=True)

    len_row = lengths[...].astype(F32)
    route_row = route[...].astype(F32)
    len_col, route_col = column(len_row), column(route_row)
    end_row = jnp.sum(jnp.where(down <= across, len_col, 0.0), axis=0, keepdims=True)
    end_col = jnp.sum(jnp.where(across <= down, len_row, 0.0), axis=1, keepdims=True)
    same = jnp.where(route_row == route_col, 1.0, 0.0)
    slot_row = jnp.sum(jnp.where(down < across, same, 0.0), axis=0, keepdims=True)
    slot_col = jnp.sum(jnp.where(across < down, same, 0.0), axis=1, keepdims=True)
    return len_row, len_col, route_row, route_col, end_row, end_col, slot_row, slot_col


def kernel(
    states, gain, lengths, route, w_in, lat_gain, w_q, w_k, w_v, w_ao, w_out, w_head, out,
    blk, wsc, wx, wxo, p_q, p_o, r1_q, r1_o, t_q, t_o, r2_q, r2_o, m_q, m_o,
    snd, arr, snd2, arr2, ctx, lat, sqs, acc, qkv, att, lw, zp, zr, packf,
    w_s, w_r, p_s, p_r, loc, x_s, x_r, a_s, a_r, c_s, c_r, q_s, q_r,
    r1_s, r1_r, r2_s, r2_r, g1_s, g1_r, g2_s, g2_r, h_s, h_r, z_s, z_r, b_s, b_r,
):
    b = lax.axis_index("byte")
    t = lax.axis_index("tensor")
    k = b % 2
    chip = b // 2
    x = chip % SIDE
    y = chip // SIDE
    far = (t - chip // 2 + NT) % NT
    up = (b, (t + 1) % NT)
    down = (b, (t + NT - 1) % NT)
    partner = (b + 1 - 2 * k, t)
    sends = []

    def rcopy(src, dst, ssem, rsem, dev):
        return pltpu.make_async_remote_copy(
            src_ref=src, dst_ref=dst, send_sem=ssem, recv_sem=rsem, device_id=dev, device_id_type=MESH
        )

    def send(src, dst, ssem, rsem, dev):
        copy = rcopy(src, dst, ssem, rsem, dev)
        copy.start()
        sends.append(copy)

    def got(dst, ssem, rsem, dev):
        rcopy(dst, dst, ssem, rsem, dev).wait_recv()

    def rows(start, size, step=16):
        return pl.ds(pl.multiple_of(start, step), size)

    bar = pltpu.get_barrier_semaphore()

    @pl.loop(1, NB)
    def _(i):
        pl.semaphore_signal(bar, inc=1, device_id=((b + i) % NB, t), device_id_type=MESH)

    @pl.loop(1, NT)
    def _(i):
        pl.semaphore_signal(bar, inc=1, device_id=(b, (t + i) % NT), device_id_type=MESH)

    g_row = lat_gain[pl.ds(b, 1), :]
    eye = iota((128, 128), 0) == iota((128, 128), 1)
    g_col = jnp.sum(jnp.where(eye, g_row, 0.0), axis=1, keepdims=True)
    half = rows(128 * k, 128, 128)
    mine = rows(W * k, W, W)
    theirs = rows(W * (1 - k), W, W)
    for m, weight in enumerate((w_q, w_k, w_v)):
        wsc[m] = (weight[...].astype(F32) * g_col).astype(BF16)

    pl.semaphore_wait(bar, NB + NT - 2)

    for m in range(3):
        send(wsc.at[m, :, theirs], wx.at[m, half, :], x_s.at[m], x_r.at[m], partner)
    send(w_ao.at[theirs, :], wxo.at[:, half], x_s.at[3], x_r.at[3], partner)

    off = rows(W * (chip % 2), W, W)

    def relay(j):
        piece = blk.at[j, half, :]
        if j < PIECES:
            source = w_in.at[rows(W * j + 128 * k, 128, 128), off]
            whole = w_in.at[pl.ds(W * j, W), off]
        else:
            cols = pl.ds(W * (j - PIECES), W)
            source = w_out.at[rows(W * (chip % 2) + 128 * k, 128, 128), cols]
            whole = w_out.at[off, cols]

        @pl.when(far == 0)
        def _():
            rcopy(source, piece, w_s.at[j, 0], w_r.at[j], up).start()
            rcopy(source, piece, w_s.at[j, 1], w_r.at[j], down).start()
            pltpu.make_async_copy(whole, blk.at[j], loc.at[j]).start()

        @pl.when(far != 0)
        def _():
            got(piece, w_s.at[j, 0], w_r.at[j], up)

            @pl.when(far <= 3)
            def _():
                rcopy(piece, piece, w_s.at[j, 0], w_r.at[j], up).start()

            @pl.when(far >= 6)
            def _():
                rcopy(piece, piece, w_s.at[j, 1], w_r.at[j], down).start()

            rcopy(piece, piece, p_s.at[j], p_r.at[j], partner).start()

    def relay_end(j):
        piece = blk.at[j, half, :]

        @pl.when(far <= 3)
        def _():
            rcopy(piece, piece, w_s.at[j, 0], w_r.at[j], up).wait_send()

        @pl.when((far == 0) | (far >= 6))
        def _():
            rcopy(piece, piece, w_s.at[j, 1], w_r.at[j], down).wait_send()

        @pl.when(far != 0)
        def _():
            rcopy(piece, piece, p_s.at[j], p_r.at[j], partner).wait_send()

    def layout(j):
        if j < PIECES:
            return j, 3 * W // 16, p_q, r1_q, t_q, r2_q, m_q
        return j - PIECES, W // 16, p_o, r1_o, t_o, r2_o, m_o

    def axes(j):
        return (x, y) if j % 2 == 0 else (y, x)

    def peer(j, first, i):
        along_x = (j % 2 == 0) == first
        px = (x + i) % SIDE if along_x else x
        py = y if along_x else (y + i) % SIDE
        return ((py * SIDE + px) * 2 + k, t)

    def product(j):
        other = blk.at[j, rows(128 * (1 - k), 128, 128), :]

        @pl.when(far == 0)
        def _():
            pltpu.make_async_copy(blk.at[j], blk.at[j], loc.at[j]).wait()

        @pl.when(far != 0)
        def _():
            got(other, p_s.at[j], p_r.at[j], partner)

        if j == 0:
            for m in range(3):
                got(wx.at[m, rows(128 * (1 - k), 128, 128), :], x_s.at[m], x_r.at[m], partner)
                wx[m, half, :] = wsc[m, :, mine]
        if j == PIECES:
            got(wxo.at[:, rows(128 * (1 - k), 128, 128)], x_s.at[3], x_r.at[3], partner)
            wxo[:, half] = w_ao[mine, :]
        n, part, p, r1, tt, r2, m_ = layout(j)
        if j < PIECES:
            for m in range(3):
                p[n, W * m : W * (m + 1), :] = mm(blk[j], wx[m]).astype(BF16)
        else:
            p[n] = mm(wxo[...], blk[j]).astype(BF16)
        u, v = axes(j)
        for i in range(1, SIDE):
            to = (u + i) % SIDE
            send(
                p.at[n, rows(4 * part * to, 4 * part), :], r1.at[n, i - 1],
                r1_s.at[j, i - 1], r1_r.at[j, i - 1], peer(j, True, i),
            )

    def first_sum(j):
        n, part, p, r1, tt, r2, m_ = layout(j)
        u, v = axes(j)
        for i in range(1, SIDE):
            got(r1.at[n, i - 1], r1_s.at[j, i - 1], r1_r.at[j, i - 1], peer(j, True, i))
        total = p[n, rows(4 * part * u, 4 * part), :].astype(F32)
        for i in range(SIDE - 1):
            total = total + r1[n, i].astype(F32)
        tt[n] = total.astype(BF16)
        for i in range(1, SIDE):
            to = (v + i) % SIDE
            send(
                tt.at[n, rows(part * to, part), :], r2.at[n, i - 1],
                r2_s.at[j, i - 1], r2_r.at[j, i - 1], peer(j, False, i),
            )

    def second_sum(j):
        n, part, p, r1, tt, r2, m_ = layout(j)
        u, v = axes(j)
        for i in range(1, SIDE):
            got(r2.at[n, i - 1], r2_s.at[j, i - 1], r2_r.at[j, i - 1], peer(j, False, i))
        total = tt[n, rows(part * v, part), :].astype(F32)
        for i in range(SIDE - 1):
            total = total + r2[n, i].astype(F32)
        own = rows(part * (4 * u + v), part)
        m_[n, k, own, :] = total.astype(BF16)
        for i in range(1, SIDE):
            send(
                m_.at[n, k, own, :], m_.at[n, k, own, :],
                g1_s.at[j, i - 1], g1_r.at[j, i - 1], peer(j, False, i),
            )

    def first_gather(j):
        n, part, p, r1, tt, r2, m_ = layout(j)
        u, v = axes(j)
        for i in range(1, SIDE):
            came = rows(part * (4 * u + (v + SIDE - i) % SIDE), part)
            got(m_.at[n, k, came, :], g1_s.at[j, i - 1], g1_r.at[j, i - 1], peer(j, False, i))
        own = rows(4 * part * u, 4 * part)
        for i in range(1, SIDE):
            send(
                m_.at[n, k, own, :], m_.at[n, k, own, :],
                g2_s.at[j, i - 1], g2_r.at[j, i - 1], peer(j, True, i),
            )

    def second_gather(j):
        n, part, p, r1, tt, r2, m_ = layout(j)
        u, v = axes(j)
        for i in range(1, SIDE):
            came = rows(4 * part * ((u + SIDE - i) % SIDE), 4 * part)
            got(m_.at[n, k, came, :], g2_s.at[j, i - 1], g2_r.at[j, i - 1], peer(j, True, i))
        send(m_.at[n, k], m_.at[n, k], h_s.at[j], h_r.at[j], partner)

    def joined(j):
        n, part, p, r1, tt, r2, m_ = layout(j)
        got(m_.at[n, 1 - k], h_s.at[j], h_r.at[j], partner)
        if j < PIECES:
            piece = ctx[:, W * j : W * (j + 1)]
            for m in range(3):
                for side in range(2):
                    cols = slice(W * side, W * (side + 1))
                    term = mm(piece, m_[n, side, W * m : W * (m + 1), :])
                    if j == 0:
                        acc[m, :, cols] = term
                    else:
                        acc[m, :, cols] = acc[m, :, cols] + term

    def pool():
        len_row, len_col, route_row, route_col, end_row, end_col, slot_row, slot_col = tables(
            lengths, route
        )
        values = states[...].astype(F32)
        scale = lax.rsqrt(jnp.mean(values * values, axis=-1, keepdims=True) + EPS)
        normed = values * scale * gain[...]
        high = normed.astype(BF16)
        low = (normed - high.astype(F32)).astype(BF16)
        n = states.shape[0]
        place = iota((lengths.shape[1], n), 1).astype(F32)
        member = onehot((place >= end_col - len_col) & (place < end_col))
        pooled = ((mm(member, high) + mm(member, low)) / len_col).astype(BF16)
        spot = iota((NB * PACK, lengths.shape[1]), 0).astype(F32)
        target = route_row * PACK + slot_row * PIECES
        packed = mm(
            onehot(spot == route_row * PACK + 2 * PIECES + slot_row),
            jnp.ones((lengths.shape[1], W), BF16),
        )
        for j in range(PIECES):
            packed = packed + mm(onehot(spot == target + j), pooled[:, W * j : W * (j + 1)])
        snd[...] = packed.astype(BF16)

    def exchange_start(src, dst, ssem, rsem):
        own = rows(PACK * b, PACK)

        @pl.loop(1, NB)
        def _(i):
            to = (b + i) % NB
            rcopy(
                src.at[rows(PACK * to, PACK), :], dst.at[own, :], ssem.at[i], rsem.at[i], (to, t)
            ).start()

        dst[own, :] = src[own, :]

    def exchange_wait(src, dst, ssem, rsem):
        @pl.loop(1, NB)
        def _(i):
            to = (b + i) % NB
            came = (b + NB - i) % NB
            copy = rcopy(
                src.at[rows(PACK * to, PACK), :], dst.at[rows(PACK * came, PACK), :],
                ssem.at[i], rsem.at[i], (to, t),
            )
            copy.wait_send()
            copy.wait_recv()

    def slots():
        slot, spot = iota((2 * NB, NB * PACK), 0), iota((2 * NB, NB * PACK), 1)
        base = (slot // 2) * PACK
        arrived = arr[...]
        own = rows(2 * NB * t, 2 * NB)
        for j in range(PIECES):
            pick = onehot(spot == base + (slot % 2) * PIECES + j)
            ctx[own, W * j : W * (j + 1)] = mm(pick, arrived).astype(BF16)
        pick = onehot(spot == base + 2 * PIECES + slot % 2)
        ctx[own, E : E + FLAGS] = mm(pick, arrived[:, :FLAGS]).astype(BF16)

    def ctx_block(plane, side):
        plane = (plane + 2 * NT) % NT
        if side is None:
            return ctx.at[rows(2 * NB * plane, 2 * NB), :]
        return ctx.at[rows(2 * NB * plane + NB * side, NB), :]

    def ctx_send(step):
        cut = step == 3
        for side, sign, dev in ((0, -1, up), (1, 1, down)):
            block = ctx_block(t + sign * step, side if cut else None)
            send(block, block, c_s.at[side, step], c_r.at[side, step], dev)

    def ctx_got(step):
        cut = step == 3
        for side, sign, dev in ((0, -1, up), (1, 1, down)):
            block = ctx_block(t + sign * (step + 1), side if cut else None)
            got(block, c_s.at[side, step], c_r.at[side, step], dev)

    def latents():
        part = mm(ctx[:, :E], w_in[...]).astype(BF16)
        lat[...] = part
        wide = part.astype(F32)
        squares = wide * wide
        high = squares.astype(BF16)
        low = (squares - high.astype(F32)).astype(BF16)
        ones = jnp.ones((8, part.shape[1]), BF16)
        sqs[t] = mm_t(ones, high) + mm_t(ones, low)

        @pl.loop(1, NT)
        def _(i):
            rcopy(sqs.at[t], sqs.at[t], q_s.at[i], q_r.at[i], (b, (t + i) % NT)).start()

    def scales():
        @pl.loop(1, NT)
        def _(i):
            copy = rcopy(
                sqs.at[t], sqs.at[(t + NT - i) % NT], q_s.at[i], q_r.at[i], (b, (t + i) % NT)
            )
            copy.wait_send()
            copy.wait_recv()

        total = sqs[0]
        for i in range(1, NT):
            total = total + sqs[i]
        scale = lax.rsqrt(total / D + EPS)
        return jnp.transpose(scale)[:, 0:1]

    def project():
        scale = scales()
        for m in range(3):
            qkv[m] = (acc[m] * scale).astype(BF16)

    def head(h):
        cols = slice(DH * h, DH * (h + 1))
        seen = mm_t(jnp.ones((8, FLAGS), BF16), ctx[:, E : E + FLAGS])[0:1, :] > 0.5
        for i in range(CTX // 128):
            lines = slice(128 * i, 128 * (i + 1))
            n = 128 * (i + 1)
            scores = mm_t(qkv[0, lines, cols], qkv[1, :n, cols]) * DH ** (-0.5)
            line, place = iota((128, n), 0) + 128 * i, iota((128, n), 1)
            allowed = ((place < line) & seen[:, :n]) | (place == line)
            scores = jnp.where(allowed, scores, -1e30)
            raised = jnp.exp(scores - jnp.max(scores, axis=-1, keepdims=True))
            weights = raised / jnp.sum(raised, axis=-1, keepdims=True)
            att[lines, cols] = mm(weights.astype(BF16), qkv[2, :n, cols]).astype(BF16)

    def z_rows(plane, start, size):
        plane = (plane + 2 * NT) % NT
        return rows(2 * NB * plane + start, size)

    def z_first(n):
        value = mm(att[:, :W], m_o[n, 0]) + mm(att[:, W:], m_o[n, 1])
        zp[n] = (value + lw[:, W * n : W * (n + 1)]).astype(BF16)
        for side, dev in ((0, up), (1, down)):
            send(
                zp.at[n, z_rows(t + 4, NB * side, NB), :], zr.at[n, side, 0, pl.ds(0, NB), :],
                z_s.at[n, side, 0], z_r.at[n, side, 0], dev,
            )

    def z_add(n, step):
        for side, sign, dev in ((0, 1, up), (1, -1, down)):
            plane = t + sign * (4 - step)
            if step == 1:
                got(zr.at[n, side, 0, pl.ds(0, NB), :], z_s.at[n, side, 0], z_r.at[n, side, 0], dev)
                place, came = z_rows(plane, NB * side, NB), zr[n, side, 0, 0:NB, :]
            else:
                got(zr.at[n, side, step - 1], z_s.at[n, side, step - 1], z_r.at[n, side, step - 1], dev)
                place, came = z_rows(plane, 0, 2 * NB), zr[n, side, step - 1]
            zp[n, place, :] = (zp[n, place, :].astype(F32) + came.astype(F32)).astype(BF16)
            send(
                zp.at[n, z_rows(plane, 0, 2 * NB), :], zr.at[n, side, step],
                z_s.at[n, side, step], z_r.at[n, side, step], dev,
            )

    def z_last(n):
        total = zp[n, z_rows(t, 0, 2 * NB), :].astype(F32)
        for side, dev in ((0, up), (1, down)):
            got(zr.at[n, side, 3], z_s.at[n, side, 3], z_r.at[n, side, 3], dev)
            total = total + zr[n, side, 3].astype(F32)
        spot, slot = iota((NB * PACK, 2 * NB), 0), iota((NB * PACK, 2 * NB), 1)
        pick = onehot(spot == (slot // 2) * PACK + (slot % 2) * PIECES + n)
        term = mm(pick, total.astype(BF16))
        if n == 0:
            packf[...] = term
        else:
            packf[...] = packf[...] + term

    def decode():
        len_row, len_col, route_row, route_col, end_row, end_col, slot_row, slot_col = tables(
            lengths, route
        )
        n = states.shape[0]
        place = iota((n, lengths.shape[1]), 0).astype(F32)
        member = onehot((place >= end_row - len_row) & (place < end_row))
        spot = iota((lengths.shape[1], NB * PACK), 1).astype(F32)
        target = route_col * PACK + slot_col * PIECES
        total = jnp.zeros((n, w_head.shape[1]), F32)
        for j in range(PIECES):
            cols = slice(W * j, W * (j + 1))
            values = mm(onehot(spot == target + j), arr2[...]).astype(BF16)
            decoded = (states[:, cols].astype(F32) + mm(member, values)).astype(BF16)
            total = total + mm(decoded, w_head[cols, :])
        out[...] = total.astype(BF16)

    relay(0)
    pool()
    exchange_start(snd, arr, a_s, a_r)
    for i in range(1, STAGES + 6):
        if i < STAGES:
            relay(i)
        if i == 2:
            exchange_wait(snd, arr, a_s, a_r)
            slots()
            ctx_send(0)
        if 3 <= i <= 5:
            ctx_got(i - 3)
            ctx_send(i - 2)
        if i == 6:
            ctx_got(3)
            latents()
        if 0 <= i - 6 < STAGES:
            joined(i - 6)
        if 0 <= i - 5 < STAGES:
            second_gather(i - 5)
        if 0 <= i - 4 < STAGES:
            first_gather(i - 4)
        if 0 <= i - 3 < STAGES:
            second_sum(i - 3)
        if 0 <= i - 2 < STAGES:
            first_sum(i - 2)
        if 0 <= i - 1 < STAGES:
            product(i - 1)
        if i == 8:
            lw[...] = mm(lat[...], w_out[...])
        if i == 10:
            project()
        if 10 <= i < 14:
            head(i - 10)
        if i == 13:
            for n in range(3):
                z_first(n)
        if i == 14:
            z_first(3)
            for n in range(3):
                z_add(n, 1)
        if i == 15:
            z_first(4)
    z_add(3, 1)
    for n in range(3):
        z_add(n, 2)
    z_add(4, 1)
    z_add(3, 2)
    for n in range(3):
        z_add(n, 3)
    z_add(4, 2)
    z_add(3, 3)
    for n in range(3):
        z_last(n)
    z_add(4, 3)
    z_last(3)
    z_last(4)
    snd2[...] = packf[...].astype(BF16)
    exchange_start(snd2, arr2, b_s, b_r)
    exchange_wait(snd2, arr2, b_s, b_r)
    decode()
    for copy in sends:
        copy.wait_send()
    for j in range(STAGES):
        relay_end(j)


def body(
    byte_states, enc_gain, patch_lengths, patch_route, w_in, latent_gain,
    w_query, w_key, w_value, w_attn_out, w_out, w_head,
):
    vmem = pl.BlockSpec(memory_space=pltpu.VMEM)
    dma = pltpu.SemaphoreType.DMA
    part_q, part_o = 3 * W // 16, W // 16

    def buf(*shape, dtype=BF16):
        return pltpu.VMEM(shape, dtype)

    scratch = [
        buf(STAGES, W, W),
        buf(3, 128, 2 * W),
        buf(3, W, W),
        buf(W, W),
        buf(PIECES, 3 * W, W),
        buf(PIECES, W, W),
        buf(PIECES, 3, 4 * part_q, W),
        buf(PIECES, 3, 4 * part_o, W),
        buf(PIECES, 4 * part_q, W),
        buf(PIECES, 4 * part_o, W),
        buf(PIECES, 3, part_q, W),
        buf(PIECES, 3, part_o, W),
        buf(PIECES, 2, 3 * W, W),
        buf(PIECES, 2, W, W),
        buf(NB * PACK, W),
        buf(NB * PACK, W),
        buf(NB * PACK, W),
        buf(NB * PACK, W),
        buf(CTX, E + FLAGS),
        buf(CTX, 2 * W),
        buf(NT, 8, CTX, dtype=F32),
        buf(3, CTX, 2 * W, dtype=F32),
        buf(3, CTX, 2 * W),
        buf(CTX, 2 * W),
        buf(CTX, E, dtype=F32),
        buf(PIECES, CTX, W),
        buf(PIECES, 2, 4, 2 * NB, W),
        buf(NB * PACK, W, dtype=F32),
        dma((STAGES, 2)), dma((STAGES,)), dma((STAGES,)), dma((STAGES,)), dma((STAGES,)),
        dma((4,)), dma((4,)), dma((NB,)), dma((NB,)), dma((2, 4)), dma((2, 4)),
        dma((NT,)), dma((NT,)),
        dma((STAGES, 3)), dma((STAGES, 3)), dma((STAGES, 3)), dma((STAGES, 3)),
        dma((STAGES, 3)), dma((STAGES, 3)), dma((STAGES, 3)), dma((STAGES, 3)),
        dma((STAGES,)), dma((STAGES,)), dma((PIECES, 2, 4)), dma((PIECES, 2, 4)),
        dma((NB,)), dma((NB,)),
    ]
    return pl.pallas_call(
        kernel,
        out_shape=jax.ShapeDtypeStruct((byte_states.shape[0], w_head.shape[1]), BF16),
        in_specs=[vmem] * 12,
        out_specs=vmem,
        scratch_shapes=scratch,
        compiler_params=pltpu.CompilerParams(
            collective_id=0, has_side_effects=True, vmem_limit_bytes=56 * 1024 * 1024
        ),
    )(
        byte_states, enc_gain.reshape(1, -1), patch_lengths, patch_route.reshape(1, -1), w_in,
        latent_gain.reshape(NB, -1), w_query, w_key, w_value, w_attn_out, w_out, w_head,
    )


def solution(mesh):
    return jax.shard_map(
        body,
        mesh=mesh,
        in_specs=(
            P(("byte", "tensor"), None),
            P(),
            P(("byte", "tensor"), None),
            P(("byte", "tensor"), None, None),
            P(None, "tensor"),
            P(),
            P("byte", "tensor"),
            P("byte", "tensor"),
            P("byte", "tensor"),
            P("tensor", "byte"),
            P("tensor", None),
            P(),
        ),
        out_specs=P(("byte", "tensor"), None),
        check_vma=False,
    )
```

```python
import jax
import jax.numpy as jnp
from jax import lax
from jax.experimental import pallas as pl
from jax.experimental.pallas import tpu as pltpu
from jax.sharding import PartitionSpec as P

MESH = pl.DeviceIdType.MESH
BF16 = jnp.bfloat16
F32 = jnp.float32
DH = 128
EPS = 1e-06
SIDE = 4
NB = 32
NT = 8
E = 1280
D = 4096
CTX = 512
W = 256
PIECES = E // W
STAGES = 2 * PIECES
FLAGS = 128
PACK = 16

ORDER = (
    ("start", 2), ("start", 3), ("start", 4), ("relay", 0, 1), ("relay", 1, 1), ("relay", 0, 2),
    ("relay", 2, 1), ("relay", 1, 2), ("exch",), ("start", 5), ("relay", 3, 1), ("relay", 0, 3),
    ("relay", 2, 2), ("relay", 4, 1), ("start", 6), ("relay", 1, 3), ("relay", 5, 1),
    ("relay", 3, 2), ("relay", 0, 4), ("relay", 2, 3), ("start", 7), ("relay", 4, 2),
    ("product", 0), ("relay", 6, 1), ("relay", 1, 4), ("relay", 5, 2), ("relay", 3, 3),
    ("start", 8), ("product", 1), ("ctx", 0), ("relay", 2, 4), ("relay", 7, 1), ("relay", 4, 3),
    ("relay", 6, 2), ("product", 2), ("turn", 0), ("start", 9), ("relay", 5, 3), ("relay", 3, 4),
    ("relay", 8, 1), ("product", 3), ("turn", 1), ("relay", 7, 2), ("relay", 4, 4), ("relay", 6, 3),
    ("relay", 9, 1), ("product", 4), ("turn", 2), ("relay", 5, 4), ("relay", 8, 2), ("product", 5),
    ("ctx", 1), ("relay", 7, 3), ("turn", 3), ("sum1", 0), ("relay", 6, 4), ("relay", 9, 2),
    ("product", 6), ("turn", 4), ("relay", 8, 3), ("sum1", 1), ("turn", 5), ("relay", 7, 4),
    ("product", 7), ("sum1", 2), ("relay", 9, 3), ("turn", 6), ("sum1", 3), ("relay", 8, 4),
    ("ctx", 2), ("product", 8), ("sum2", 0), ("sum1", 4), ("sum1", 5), ("turn", 7), ("relay", 9, 4),
    ("sum2", 1), ("product", 9), ("sum2", 2), ("sum1", 6), ("gather1", 0), ("sum2", 3), ("ctx", 3),
    ("lat",), ("turn", 8), ("sum2", 5), ("sum2", 4), ("sum1", 7), ("gather1", 1), ("turn", 9),
    ("gather1", 2), ("sum2", 6), ("gather2", 0), ("res",), ("gather1", 4), ("gather1", 3),
    ("sum1", 8), ("gather1", 5), ("sum2", 7), ("gather2", 1), ("sum1", 9), ("gather1", 6),
    ("gather2", 2), ("gather3", 0), ("gather2", 3), ("sum2", 8), ("gather2", 5), ("joined", 0),
    ("gather2", 4), ("gather1", 7), ("gather3", 1), ("sum2", 9), ("gather2", 6), ("gather3", 3),
    ("gather1", 8), ("gather3", 5), ("joined", 1), ("gather3", 2), ("gather2", 7), ("joined", 3),
    ("gather3", 4), ("joined", 5), ("gather1", 9), ("gather3", 6), ("joined", 2), ("gather2", 8),
    ("gather3", 7), ("joined", 4), ("joined", 6), ("proj",), ("gather2", 9), ("joined", 7),
    ("head", 0), ("gather3", 8), ("head", 1), ("gather3", 9), ("joined", 8), ("head", 2),
    ("joined", 9), ("head", 3), ("zf", 0), ("zf", 1), ("zf", 2), ("zf", 3), ("zf", 4), ("za", 0, 1),
    ("za", 1, 1), ("za", 2, 1), ("za", 3, 1), ("za", 4, 1), ("za", 0, 2), ("za", 1, 2),
    ("za", 2, 2), ("za", 3, 2), ("za", 4, 2), ("za", 0, 3), ("za", 1, 3), ("za", 2, 3),
    ("za", 3, 3), ("za", 4, 3), ("zl", 0), ("zl", 1), ("zl", 2), ("zl", 3), ("zl", 4),
)


def mm(a, b):
    return jnp.dot(a, b, preferred_element_type=F32)


def mm_t(a, b):
    return lax.dot_general(a, b, (((1,), (1,)), ((), ())), preferred_element_type=F32)


def iota(shape, dim):
    return lax.broadcasted_iota(jnp.int32, shape, dim)


def onehot(mask):
    return jnp.where(mask, 1.0, 0.0).astype(BF16)


def tables(lengths, route):
    n = lengths.shape[1]
    down, across = iota((n, n), 0), iota((n, n), 1)
    eye = down == across

    def column(row):
        return jnp.sum(jnp.where(eye, row, 0.0), axis=1, keepdims=True)

    len_row = lengths[...].astype(F32)
    route_row = route[...].astype(F32)
    len_col, route_col = column(len_row), column(route_row)
    end_row = jnp.sum(jnp.where(down <= across, len_col, 0.0), axis=0, keepdims=True)
    end_col = jnp.sum(jnp.where(across <= down, len_row, 0.0), axis=1, keepdims=True)
    same = jnp.where(route_row == route_col, 1.0, 0.0)
    slot_row = jnp.sum(jnp.where(down < across, same, 0.0), axis=0, keepdims=True)
    slot_col = jnp.sum(jnp.where(across < down, same, 0.0), axis=1, keepdims=True)
    return len_row, len_col, route_row, route_col, end_row, end_col, slot_row, slot_col


def kernel(
    states, gain, lengths, route, w_in, lat_gain, w_q, w_k, w_v, w_ao, w_out, w_head, out,
    blk, wsc, wx, wxo, p_q, p_o, a1_q, a1_o, b1_q, b1_o, t_q, t_o, r2_q, r2_o, m_q, m_o,
    snd, arr, snd2, arr2, ctx, lat, sqs, acc, qkv, att, lw, zp, zr, packf,
    w_s, w_r, p_s, p_r, loc, x_s, x_r, a_s, a_r, c_s, c_r, q_s, q_r,
    sum_s, a1_r, b1_r, r2_r, g1_r, g2_r, g3_r, h_r, z_s, z_r, b_s, b_r,
):
    b = lax.axis_index("byte")
    t = lax.axis_index("tensor")
    k = b % 2
    chip = b // 2
    x = chip % SIDE
    y = chip // SIDE
    far = (t - chip // 2 + NT) % NT
    up = (b, (t + 1) % NT)
    down = (b, (t + NT - 1) % NT)
    partner = (b + 1 - 2 * k, t)

    def rcopy(src, dst, ssem, rsem, dev):
        return pltpu.make_async_remote_copy(
            src_ref=src, dst_ref=dst, send_sem=ssem, recv_sem=rsem, device_id=dev, device_id_type=MESH
        )

    def send(src, dst, ssem, rsem, dev):
        rcopy(src, dst, ssem, rsem, dev).start()

    def got(dst, rsem):
        rcopy(dst, dst, rsem, rsem, partner).wait_recv()

    def sent(src, ssem):
        rcopy(src, src, ssem, ssem, partner).wait_send()

    def rows(start, size, step=16):
        return pl.ds(pl.multiple_of(start, step), size)

    bar = pltpu.get_barrier_semaphore()
    half = rows(128 * k, 128, 128)
    mine = rows(W * k, W, W)
    theirs = rows(W * (1 - k), W, W)

    def greet():
        @pl.loop(1, NB)
        def _(i):
            pl.semaphore_signal(bar, inc=1, device_id=((b + i) % NB, t), device_id_type=MESH)

        @pl.loop(1, NT)
        def _(i):
            pl.semaphore_signal(bar, inc=1, device_id=(b, (t + i) % NT), device_id_type=MESH)

    def scale_weights():
        g_row = lat_gain[pl.ds(b, 1), :]
        eye = iota((128, 128), 0) == iota((128, 128), 1)
        g_col = jnp.sum(jnp.where(eye, g_row, 0.0), axis=1, keepdims=True)
        for m, weight in enumerate((w_q, w_k, w_v)):
            wsc[m] = (weight[...].astype(F32) * g_col).astype(BF16)

    def meet():
        pl.semaphore_wait(bar, NB + NT - 2)

    def swap_weights():
        for m in range(3):
            send(wsc.at[m, :, theirs], wx.at[m, half, :], x_s.at[0], x_r.at[0], partner)
        send(w_ao.at[theirs, :], wxo.at[:, half], x_s.at[1], x_r.at[1], partner)

    off = rows(W * (chip % 2), W, W)

    def start(j):
        piece = blk.at[j, half, :]
        if j < PIECES:
            source = w_in.at[rows(W * j + 128 * k, 128, 128), off]
            whole = w_in.at[pl.ds(W * j, W), off]
        else:
            cols = pl.ds(W * (j - PIECES), W)
            source = w_out.at[rows(W * (chip % 2) + 128 * k, 128, 128), cols]
            whole = w_out.at[off, cols]

        @pl.when(far == 0)
        def _():
            send(source, piece, w_s.at[0], w_r.at[j], up)
            send(source, piece, w_s.at[1], w_r.at[j], down)
            pltpu.make_async_copy(whole, blk.at[j], loc.at[j]).start()

    def relay(j, hops):
        piece = blk.at[j, half, :]

        @pl.when(far == hops)
        def _():
            got(piece, w_r.at[j])
            if hops < NT // 2:
                send(piece, piece, w_s.at[0], w_r.at[j], up)
            send(piece, piece, p_s, p_r.at[j], partner)

        if hops < NT // 2:

            @pl.when(far == NT - hops)
            def _():
                got(piece, w_r.at[j])
                if hops < NT // 2 - 1:
                    send(piece, piece, w_s.at[1], w_r.at[j], down)
                send(piece, piece, p_s, p_r.at[j], partner)

    def relay_end():
        pieces = blk.at[:, half, :]

        @pl.when(far <= 3)
        def _():
            sent(pieces, w_s.at[0])

        @pl.when((far == 0) | (far >= 6))
        def _():
            sent(pieces, w_s.at[1])

        @pl.when(far != 0)
        def _():
            sent(pieces, p_s)

    def layout(j):
        if j < PIECES:
            return j, 3 * W // 16, (p_q, a1_q, b1_q, t_q, r2_q, m_q), 0
        return j - PIECES, W // 16, (p_o, a1_o, b1_o, t_o, r2_o, m_o), 1

    def axes(j):
        return (x, y) if j % 2 == 0 else (y, x)

    def peer(j, first, i):
        along_x = (j % 2 == 0) == first
        px = (x + i) % SIDE if along_x else x
        py = y if along_x else (y + i) % SIDE
        return ((py * SIDE + px) * 2 + k, t)

    def product(j):
        other = rows(128 * (1 - k), 128, 128)

        @pl.when(far == 0)
        def _():
            pltpu.make_async_copy(blk.at[j], blk.at[j], loc.at[j]).wait()

        @pl.when(far != 0)
        def _():
            got(blk.at[j, other, :], p_r.at[j])

        if j == 0:
            got(wx.at[:, other, :], x_r.at[0])
            for m in range(3):
                wx[m, half, :] = wsc[m, :, mine]
        if j == PIECES:
            got(wxo.at[:, other], x_r.at[1])
            wxo[:, half] = w_ao[mine, :]
        n, part, (p, a1, b1, tt, r2, m_), kind = layout(j)
        if j < PIECES:
            for m in range(3):
                p[n, W * m : W * (m + 1), :] = mm(blk[j], wx[m]).astype(BF16)
        else:
            p[n] = mm(wxo[...], blk[j]).astype(BF16)
        u, v = axes(j)
        for side, way in ((0, 1), (1, SIDE - 1)):
            block = rows(4 * part * ((u + 2) % SIDE) + 2 * part * side, 2 * part)
            send(
                p.at[n, block, :], a1.at[n, side],
                sum_s.at[0, kind], a1_r.at[j], peer(j, True, way),
            )

    def turn(j):
        n, part, (p, a1, b1, tt, r2, m_), kind = layout(j)
        u, v = axes(j)
        got(a1.at[n], a1_r.at[j])
        for side, way in ((0, 1), (1, SIDE - 1)):
            base = 4 * part * ((u + way) % SIDE)
            cut = rows(base + 2 * part * side, 2 * part)
            p[n, cut, :] = (p[n, cut, :].astype(F32) + a1[n, side].astype(F32)).astype(BF16)
            send(
                p.at[n, rows(base, 4 * part), :], b1.at[n, side],
                sum_s.at[1, kind], b1_r.at[j], peer(j, True, way),
            )

    def sum1(j):
        n, part, (p, a1, b1, tt, r2, m_), kind = layout(j)
        u, v = axes(j)
        got(b1.at[n], b1_r.at[j])
        total = p[n, rows(4 * part * u, 4 * part), :].astype(F32)
        total = total + b1[n, 0].astype(F32) + b1[n, 1].astype(F32)
        tt[n] = total.astype(BF16)
        for i in range(1, SIDE):
            to = (v + i) % SIDE
            send(
                tt.at[n, rows(part * to, part), :], r2.at[n, i - 1],
                sum_s.at[2, kind], r2_r.at[j], peer(j, False, i),
            )

    def sum2(j):
        n, part, (p, a1, b1, tt, r2, m_), kind = layout(j)
        u, v = axes(j)
        got(r2.at[n], r2_r.at[j])
        total = tt[n, rows(part * v, part), :].astype(F32)
        for i in range(SIDE - 1):
            total = total + r2[n, i].astype(F32)
        own = rows(part * (4 * u + v), part)
        m_[n, k, own, :] = total.astype(BF16)
        for i in range(1, SIDE):
            send(
                m_.at[n, k, own, :], m_.at[n, k, own, :],
                sum_s.at[3, kind], g1_r.at[j], peer(j, False, i),
            )

    def gather1(j):
        n, part, (p, a1, b1, tt, r2, m_), kind = layout(j)
        u, v = axes(j)
        got(r2.at[n], g1_r.at[j])
        own = rows(4 * part * u, 4 * part)
        for way in (1, SIDE - 1):
            send(
                m_.at[n, k, own, :], m_.at[n, k, own, :],
                sum_s.at[4, kind], g2_r.at[j], peer(j, True, way),
            )

    def gather2(j):
        n, part, (p, a1, b1, tt, r2, m_), kind = layout(j)
        u, v = axes(j)
        got(b1.at[n], g2_r.at[j])
        for side, way in ((0, 1), (1, SIDE - 1)):
            base = 4 * part * ((u + SIDE - way) % SIDE) + 2 * part * side
            block = m_.at[n, k, rows(base, 2 * part), :]
            send(block, block, sum_s.at[5, kind], g3_r.at[j], peer(j, True, way))

    def gather3(j):
        n, part, (p, a1, b1, tt, r2, m_), kind = layout(j)
        got(a1.at[n], g3_r.at[j])
        send(m_.at[n, k], m_.at[n, k], sum_s.at[6, kind], h_r.at[j], partner)

    def joined(j):
        n, part, (p, a1, b1, tt, r2, m_), kind = layout(j)
        got(m_.at[n, 1 - k], h_r.at[j])
        if j < PIECES:
            piece = ctx[:, W * j : W * (j + 1)]
            for m in range(3):
                for side in range(2):
                    cols = slice(W * side, W * (side + 1))
                    term = mm(piece, m_[n, side, W * m : W * (m + 1), :])
                    if j == 0:
                        acc[m, :, cols] = term
                    else:
                        acc[m, :, cols] = acc[m, :, cols] + term

    def sums_end():
        for kind in range(2):
            p, a1, b1, tt, r2, m_ = layout(kind * PIECES)[2]
            for i, ref in enumerate((a1, b1, r2, r2, b1, a1)):
                sent(ref, sum_s.at[i, kind])
            sent(m_.at[:, 0], sum_s.at[6, kind])

    def pool():
        len_row, len_col, route_row, route_col, end_row, end_col, slot_row, slot_col = tables(
            lengths, route
        )
        values = states[...].astype(F32)
        scale = lax.rsqrt(jnp.mean(values * values, axis=-1, keepdims=True) + EPS)
        normed = values * scale * gain[...]
        high = normed.astype(BF16)
        low = (normed - high.astype(F32)).astype(BF16)
        n = states.shape[0]
        place = iota((lengths.shape[1], n), 1).astype(F32)
        member = onehot((place >= end_col - len_col) & (place < end_col))
        pooled = ((mm(member, high) + mm(member, low)) / len_col).astype(BF16)
        spot = iota((NB * PACK, lengths.shape[1]), 0).astype(F32)
        target = route_row * PACK + slot_row * PIECES
        packed = mm(
            onehot(spot == route_row * PACK + 2 * PIECES + slot_row),
            jnp.ones((lengths.shape[1], W), BF16),
        )
        for j in range(PIECES):
            packed = packed + mm(onehot(spot == target + j), pooled[:, W * j : W * (j + 1)])
        snd[...] = packed.astype(BF16)

    def exchange_start(src, dst, ssem, rsem):
        own = rows(PACK * b, PACK)

        @pl.loop(1, NB)
        def _(i):
            to = (b + i) % NB
            send(src.at[rows(PACK * to, PACK), :], dst.at[own, :], ssem, rsem, (to, t))

        dst[own, :] = src[own, :]

    def exchange_wait(src, dst, ssem, rsem):
        most = pl.ds(0, (NB - 1) * PACK)
        sent(src.at[most, :], ssem)
        got(dst.at[most, :], rsem)

    def slots():
        slot, spot = iota((2 * NB, NB * PACK), 0), iota((2 * NB, NB * PACK), 1)
        base = (slot // 2) * PACK
        arrived = arr[...]
        own = rows(2 * NB * t, 2 * NB)
        for j in range(PIECES):
            pick = onehot(spot == base + (slot % 2) * PIECES + j)
            ctx[own, W * j : W * (j + 1)] = mm(pick, arrived).astype(BF16)
        pick = onehot(spot == base + 2 * PIECES + slot % 2)
        ctx[own, E : E + FLAGS] = mm(pick, arrived[:, :FLAGS]).astype(BF16)

    def ctx_block(plane, side):
        plane = (plane + 2 * NT) % NT
        if side is None:
            return ctx.at[rows(2 * NB * plane, 2 * NB), :]
        return ctx.at[rows(2 * NB * plane + NB * side, NB), :]

    def ctx_send(step):
        cut = step == 3
        for side, sign, dev in ((0, -1, up), (1, 1, down)):
            block = ctx_block(t + sign * step, side if cut else None)
            send(block, block, c_s.at[side], c_r.at[side, step], dev)

    def ctx_got(step):
        cut = step == 3
        for side, sign, dev in ((0, -1, up), (1, 1, down)):
            block = ctx_block(t + sign * (step + 1), side if cut else None)
            got(block, c_r.at[side, step])

    def ctx_end():
        for side in range(2):
            sent(ctx.at[pl.ds(0, 7 * NB), :], c_s.at[side])

    def latents():
        part = mm(ctx[:, :E], w_in[...]).astype(BF16)
        lat[...] = part
        wide = part.astype(F32)
        squares = wide * wide
        high = squares.astype(BF16)
        low = (squares - high.astype(F32)).astype(BF16)
        ones = jnp.ones((8, part.shape[1]), BF16)
        sqs[t] = mm_t(ones, high) + mm_t(ones, low)

        @pl.loop(1, NT)
        def _(i):
            send(sqs.at[t], sqs.at[t], q_s, q_r, (b, (t + i) % NT))

    def scales():
        most = sqs.at[pl.ds(0, NT - 1)]
        sent(most, q_s)
        got(most, q_r)
        total = sqs[0]
        for i in range(1, NT):
            total = total + sqs[i]
        scale = lax.rsqrt(total / D + EPS)
        return jnp.transpose(scale)[:, 0:1]

    def project():
        scale = scales()
        for m in range(3):
            qkv[m] = (acc[m] * scale).astype(BF16)

    def head(h):
        cols = slice(DH * h, DH * (h + 1))
        seen = mm_t(jnp.ones((8, FLAGS), BF16), ctx[:, E : E + FLAGS])[0:1, :] > 0.5
        for i in range(CTX // 128):
            lines = slice(128 * i, 128 * (i + 1))
            n = 128 * (i + 1)
            scores = mm_t(qkv[0, lines, cols], qkv[1, :n, cols]) * DH ** (-0.5)
            line, place = iota((128, n), 0) + 128 * i, iota((128, n), 1)
            allowed = ((place < line) & seen[:, :n]) | (place == line)
            scores = jnp.where(allowed, scores, -1e30)
            raised = jnp.exp(scores - jnp.max(scores, axis=-1, keepdims=True))
            weights = raised / jnp.sum(raised, axis=-1, keepdims=True)
            att[lines, cols] = mm(weights.astype(BF16), qkv[2, :n, cols]).astype(BF16)

    def z_rows(plane, start, size):
        plane = (plane + 2 * NT) % NT
        return rows(2 * NB * plane + start, size)

    def z_first(n):
        value = mm(att[:, :W], m_o[n, 0]) + mm(att[:, W:], m_o[n, 1])
        zp[n] = (value + lw[:, W * n : W * (n + 1)]).astype(BF16)
        for side, dev in ((0, up), (1, down)):
            send(
                zp.at[n, z_rows(t + 4, NB * side, NB), :], zr.at[n, 0, side, pl.ds(0, NB), :],
                z_s.at[0], z_r.at[n, 0], dev,
            )

    def z_add(n, step):
        if step == 1:
            got(zr.at[n, 0, :, pl.ds(0, NB), :], z_r.at[n, 0])
        else:
            got(zr.at[n, step - 1], z_r.at[n, step - 1])
        for side, sign, dev in ((0, 1, up), (1, -1, down)):
            plane = t + sign * (4 - step)
            if step == 1:
                place, came = z_rows(plane, NB * side, NB), zr[n, 0, side, 0:NB, :]
            else:
                place, came = z_rows(plane, 0, 2 * NB), zr[n, step - 1, side]
            zp[n, place, :] = (zp[n, place, :].astype(F32) + came.astype(F32)).astype(BF16)
            send(
                zp.at[n, z_rows(plane, 0, 2 * NB), :], zr.at[n, step, side],
                z_s.at[1], z_r.at[n, step], dev,
            )

    def z_last(n):
        got(zr.at[n, 3], z_r.at[n, 3])
        total = zp[n, z_rows(t, 0, 2 * NB), :].astype(F32)
        total = total + zr[n, 3, 0].astype(F32) + zr[n, 3, 1].astype(F32)
        spot, slot = iota((NB * PACK, 2 * NB), 0), iota((NB * PACK, 2 * NB), 1)
        pick = onehot(spot == (slot // 2) * PACK + (slot % 2) * PIECES + n)
        term = mm(pick, total.astype(BF16))
        if n == 0:
            packf[...] = term
        else:
            packf[...] = packf[...] + term

    def z_end():
        sent(zr.at[:, 0, :, pl.ds(0, NB), :], z_s.at[0])
        sent(zr.at[:, pl.ds(1, 3)], z_s.at[1])

    def decode():
        len_row, len_col, route_row, route_col, end_row, end_col, slot_row, slot_col = tables(
            lengths, route
        )
        n = states.shape[0]
        place = iota((n, lengths.shape[1]), 0).astype(F32)
        member = onehot((place >= end_row - len_row) & (place < end_row))
        spot = iota((lengths.shape[1], NB * PACK), 1).astype(F32)
        target = route_col * PACK + slot_col * PIECES
        total = jnp.zeros((n, w_head.shape[1]), F32)
        for j in range(PIECES):
            cols = slice(W * j, W * (j + 1))
            values = mm(onehot(spot == target + j), arr2[...]).astype(BF16)
            decoded = (states[:, cols].astype(F32) + mm(member, values)).astype(BF16)
            total = total + mm(decoded, w_head[cols, :])
        out[...] = total.astype(BF16)

    def add_residual():
        lw[...] = mm(lat[...], w_out[...])

    def exch():
        exchange_wait(snd, arr, a_s, a_r)
        slots()
        ctx_send(0)

    def ctx_step(step):
        ctx_got(step)
        if step < 3:
            ctx_send(step + 1)

    def finish():
        sent(wsc.at[:, :, theirs], x_s.at[0])
        sent(wxo.at[:, half], x_s.at[1])
        relay_end()
        ctx_end()
        sums_end()
        z_end()

    stages = {
        "start": start, "relay": relay, "product": product, "turn": turn, "sum1": sum1,
        "sum2": sum2, "gather1": gather1, "gather2": gather2, "gather3": gather3,
        "joined": joined, "exch": exch, "ctx": ctx_step, "lat": latents, "res": add_residual,
        "proj": project, "head": head, "zf": z_first, "za": z_add, "zl": z_last,
    }
    greet()
    scale_weights()
    pool()
    meet()
    swap_weights()
    start(0)
    start(1)
    exchange_start(snd, arr, a_s, a_r)
    for name, *where in ORDER:
        stages[name](*where)
    snd2[...] = packf[...].astype(BF16)
    exchange_start(snd2, arr2, b_s, b_r)
    exchange_wait(snd2, arr2, b_s, b_r)
    decode()
    finish()


def body(
    byte_states, enc_gain, patch_lengths, patch_route, w_in, latent_gain,
    w_query, w_key, w_value, w_attn_out, w_out, w_head,
):
    vmem = pl.BlockSpec(memory_space=pltpu.VMEM)
    dma = pltpu.SemaphoreType.DMA
    part_q, part_o = 3 * W // 16, W // 16

    def buf(*shape, dtype=BF16):
        return pltpu.VMEM(shape, dtype)

    scratch = [
        buf(STAGES, W, W),
        buf(3, 128, 2 * W),
        buf(3, W, W),
        buf(W, W),
        buf(PIECES, 3 * W, W),
        buf(PIECES, W, W),
        buf(PIECES, 2, 2 * part_q, W),
        buf(PIECES, 2, 2 * part_o, W),
        buf(PIECES, 2, 4 * part_q, W),
        buf(PIECES, 2, 4 * part_o, W),
        buf(PIECES, 4 * part_q, W),
        buf(PIECES, 4 * part_o, W),
        buf(PIECES, 3, part_q, W),
        buf(PIECES, 3, part_o, W),
        buf(PIECES, 2, 3 * W, W),
        buf(PIECES, 2, W, W),
        buf(NB * PACK, W),
        buf(NB * PACK, W),
        buf(NB * PACK, W),
        buf(NB * PACK, W),
        buf(CTX, E + FLAGS),
        buf(CTX, 2 * W),
        buf(NT, 8, CTX, dtype=F32),
        buf(3, CTX, 2 * W, dtype=F32),
        buf(3, CTX, 2 * W),
        buf(CTX, 2 * W),
        buf(CTX, E, dtype=F32),
        buf(PIECES, CTX, W),
        buf(PIECES, 4, 2, 2 * NB, W),
        buf(NB * PACK, W, dtype=F32),
        dma((2,)), dma((STAGES,)), dma, dma((STAGES,)), dma((STAGES,)),
        dma((2,)), dma((2,)), dma, dma, dma((2,)), dma((2, 4)), dma, dma,
        dma((7, 2)),
        dma((STAGES,)), dma((STAGES,)), dma((STAGES,)), dma((STAGES,)), dma((STAGES,)),
        dma((STAGES,)), dma((STAGES,)),
        dma((2,)), dma((PIECES, 4)), dma, dma,
    ]
    return pl.pallas_call(
        kernel,
        out_shape=jax.ShapeDtypeStruct((byte_states.shape[0], w_head.shape[1]), BF16),
        in_specs=[vmem] * 12,
        out_specs=vmem,
        scratch_shapes=scratch,
        compiler_params=pltpu.CompilerParams(
            collective_id=0, has_side_effects=True, vmem_limit_bytes=56 * 1024 * 1024
        ),
    )(
        byte_states, enc_gain.reshape(1, -1), patch_lengths, patch_route.reshape(1, -1), w_in,
        latent_gain.reshape(NB, -1), w_query, w_key, w_value, w_attn_out, w_out, w_head,
    )


def solution(mesh):
    return jax.shard_map(
        body,
        mesh=mesh,
        in_specs=(
            P(("byte", "tensor"), None),
            P(),
            P(("byte", "tensor"), None),
            P(("byte", "tensor"), None, None),
            P(None, "tensor"),
            P(),
            P("byte", "tensor"),
            P("byte", "tensor"),
            P("byte", "tensor"),
            P("tensor", "byte"),
            P("tensor", None),
            P(),
        ),
        out_specs=P(("byte", "tensor"), None),
        check_vma=False,
    )
```

```python
import jax
import jax.numpy as jnp
from jax import lax
from jax.experimental import pallas as pl
from jax.experimental.pallas import tpu as pltpu
from jax.sharding import PartitionSpec as P

MESH = pl.DeviceIdType.MESH
BF16 = jnp.bfloat16
F32 = jnp.float32
DH = 128
EPS = 1e-06
LOG2E = 1.4426950408889634
SIDE = 4
NB = 32
NT = 8
E = 1280
D = 4096
CTX = 512
W = 256
PIECES = E // W
STAGES = 2 * PIECES
FLAGS = 128
PACK = 16

ORDER = (
    ("start", 2), ("start", 3), ("start", 4), ("relay", 0, 1), ("relay", 1, 1), ("relay", 0, 2),
    ("relay", 2, 1), ("relay", 1, 2), ("relay", 3, 1), ("exch",), ("relay", 0, 3), ("start", 5),
    ("relay", 2, 2), ("relay", 4, 1), ("relay", 1, 3), ("start", 6), ("relay", 3, 2),
    ("relay", 0, 4), ("relay", 5, 1), ("relay", 2, 3), ("start", 7), ("relay", 4, 2),
    ("product", 0), ("relay", 1, 4), ("relay", 6, 1), ("relay", 3, 3), ("start", 8), ("product", 1),
    ("relay", 5, 2), ("relay", 2, 4), ("relay", 7, 1), ("relay", 4, 3), ("product", 2),
    ("start", 9), ("relay", 6, 2), ("relay", 3, 4), ("turn", 0), ("relay", 8, 1), ("relay", 5, 3),
    ("product", 3), ("relay", 7, 2), ("relay", 4, 4), ("turn", 1), ("relay", 9, 1), ("relay", 6, 3),
    ("product", 4), ("relay", 8, 2), ("turn", 2), ("relay", 5, 4), ("relay", 7, 3), ("relay", 9, 2),
    ("turn", 3), ("relay", 6, 4), ("product", 5), ("sum1", 0), ("relay", 8, 3), ("turn", 4),
    ("relay", 7, 4), ("product", 6), ("sum1", 1), ("relay", 9, 3), ("ctxgo",), ("relay", 8, 4),
    ("product", 7), ("sum1", 2), ("sum1", 3), ("relay", 9, 4), ("product", 8), ("sum1", 5),
    ("ctx", 0, 0), ("sum1", 4), ("product", 9), ("sum2", 0), ("sum1", 6), ("ctx", 0, 1),
    ("sum1", 7), ("sum2", 1), ("own",), ("sum2", 2), ("sum2", 3), ("ctx", 1, 0), ("sum2", 4),
    ("sum1", 8), ("sum2", 5), ("sum2", 7), ("ctx", 1, 1), ("sum1", 9), ("gather1", 1),
    ("gather1", 0), ("sum2", 6), ("gather1", 3), ("gather1", 5), ("ctx", 2, 0), ("gather1", 2),
    ("gather1", 7), ("gather1", 4), ("sum2", 8), ("sum2", 9), ("ctx", 2, 1), ("ctx", 3, 0),
    ("gather2", 1), ("gather2", 0), ("gather1", 6), ("ctx", 3, 1), ("gather2", 2), ("gather2", 3),
    ("lat",), ("mask",), ("gather3", 5), ("gather2", 4), ("gather1", 9), ("gather3", 7),
    ("gather1", 8), ("gather3", 0), ("joined", 5), ("joined", 7), ("gather3", 1), ("res",),
    ("gather3", 6), ("gather3", 3), ("joined", 0), ("gather3", 2), ("joined", 1), ("gather3", 9),
    ("gather3", 4), ("joined", 6), ("joined", 3), ("gather3", 8), ("joined", 2), ("joined", 9),
    ("joined", 4), ("joined", 8), ("proj",), ("head", 0), ("head", 1), ("head", 2), ("head", 3),
    ("zf", 0), ("zf", 1), ("zf", 2), ("zf", 3), ("zf", 4), ("za", 0, 1), ("za", 1, 1), ("za", 2, 1),
    ("za", 3, 1), ("za", 4, 1), ("za", 0, 2), ("za", 1, 2), ("za", 2, 2), ("za", 3, 2),
    ("za", 4, 2), ("za", 0, 3), ("za", 1, 3), ("za", 2, 3), ("za", 3, 3), ("za", 4, 3), ("zl", 0),
    ("zl", 1), ("zl", 2), ("zl", 3), ("zl", 4),
)


def mm(a, b):
    return jnp.dot(a, b, preferred_element_type=F32)


def mm_t(a, b):
    return lax.dot_general(a, b, (((1,), (1,)), ((), ())), preferred_element_type=F32)


def iota(shape, dim):
    return lax.broadcasted_iota(jnp.int32, shape, dim)


def onehot(mask):
    return jnp.where(mask, 1.0, 0.0).astype(BF16)


def tables(lengths, route):
    n = lengths.shape[1]
    down, across = iota((n, n), 0), iota((n, n), 1)
    eye = down == across

    def column(row):
        return jnp.sum(jnp.where(eye, row, 0.0), axis=1, keepdims=True)

    len_row = lengths[...].astype(F32)
    route_row = route[...].astype(F32)
    len_col, route_col = column(len_row), column(route_row)
    end_row = jnp.sum(jnp.where(down <= across, len_col, 0.0), axis=0, keepdims=True)
    end_col = jnp.sum(jnp.where(across <= down, len_row, 0.0), axis=1, keepdims=True)
    same = jnp.where(route_row == route_col, 1.0, 0.0)
    slot_row = jnp.sum(jnp.where(down < across, same, 0.0), axis=0, keepdims=True)
    slot_col = jnp.sum(jnp.where(across < down, same, 0.0), axis=1, keepdims=True)
    return len_row, len_col, route_row, route_col, end_row, end_col, slot_row, slot_col


def kernel(
    states_far, gain_far, lengths_far, route_far, w_in_far, lat_gain_far,
    w_q_far, w_k_far, w_v_far, w_ao_far, w_out_far, w_head_far, out,
    states, gain, lengths, route, w_in, lat_gain, w_q, w_k, w_v, w_ao, w_out, w_head, in_s,
    blk, wsc, wx, wxo, p_q, p_o, a1_q, b1_q, r1_o, t_q, t_o, r2_q, r2_o, m_q, m_o,
    snd, arr, snd2, arr2, ctx, lat, sqs, acc, qk, vals, bias, base, att, lw, zp, zr, packf,
    w_s, w_r, p_s, p_r, loc, x_s, x_r, a_s, a_r, c_s, c_r, q_s, q_r,
    sum_s, a1_r, b1_r, r2_r, g1_r, g2_r, g3_r, h_r, z_s, z_r, b_s, b_r,
):
    b = lax.axis_index("byte")
    t = lax.axis_index("tensor")
    k = b % 2
    chip = b // 2
    x = chip % SIDE
    y = chip // SIDE
    far = (t - chip // 2 + NT) % NT
    up = (b, (t + 1) % NT)
    down = (b, (t + NT - 1) % NT)
    partner = (b + 1 - 2 * k, t)

    def rcopy(src, dst, ssem, rsem, dev):
        return pltpu.make_async_remote_copy(
            src_ref=src, dst_ref=dst, send_sem=ssem, recv_sem=rsem, device_id=dev, device_id_type=MESH
        )

    def send(src, dst, ssem, rsem, dev):
        rcopy(src, dst, ssem, rsem, dev).start()

    def got(dst, rsem):
        rcopy(dst, dst, rsem, rsem, partner).wait_recv()

    def sent(src, ssem):
        rcopy(src, src, ssem, ssem, partner).wait_send()

    def rows(start, size, step=16):
        return pl.ds(pl.multiple_of(start, step), size)

    bar = pltpu.get_barrier_semaphore()
    half = rows(128 * k, 128, 128)
    mine = rows(W * k, W, W)
    theirs = rows(W * (1 - k), W, W)

    def greet():
        @pl.loop(1, NB)
        def _(i):
            pl.semaphore_signal(bar, inc=1, device_id=((b + i) % NB, t), device_id_type=MESH)

        @pl.loop(1, NT)
        def _(i):
            pl.semaphore_signal(bar, inc=1, device_id=(b, (t + i) % NT), device_id_type=MESH)

    def scale_weights():
        g_row = lat_gain[pl.ds(b, 1), :]
        eye = iota((128, 128), 0) == iota((128, 128), 1)
        g_col = jnp.sum(jnp.where(eye, g_row, 0.0), axis=1, keepdims=True)
        for m, weight in enumerate((w_q, w_k, w_v)):
            wsc[m] = (weight[...].astype(F32) * g_col).astype(BF16)

    loads = {
        "gain": (lat_gain_far, lat_gain), "scale": (gain_far, gain), "lengths": (lengths_far, lengths),
        "route": (route_far, route), "states": (states_far, states), "q": (w_q_far, w_q),
        "k": (w_k_far, w_k), "v": (w_v_far, w_v), "ao": (w_ao_far, w_ao), "in": (w_in_far, w_in),
        "out": (w_out_far, w_out), "head": (w_head_far, w_head),
    }
    places = {name: i for i, name in enumerate(loads)}

    def load_start():
        for name, (src, dst) in loads.items():
            pltpu.make_async_copy(src, dst, in_s.at[places[name]]).start()

    def load_wait(*names):
        for name in names:
            src, dst = loads[name]
            pltpu.make_async_copy(src, dst, in_s.at[places[name]]).wait()

    def meet():
        pl.semaphore_wait(bar, NB + NT - 2)

    def swap_weights():
        for m in range(3):
            send(wsc.at[m, :, theirs], wx.at[m, half, :], x_s.at[0], x_r.at[0], partner)
        send(w_ao.at[theirs, :], wxo.at[:, half], x_s.at[1], x_r.at[1], partner)

    off = rows(W * (chip % 2), W, W)

    def cuts(j):
        return [rows(128 * k + 64 * i, 64, 64) for i in range(2)]

    def start(j):
        if j < PIECES:
            whole = w_in_far.at[pl.ds(W * j, W), off]
        else:
            whole = w_out_far.at[off, pl.ds(W * (j - PIECES), W)]

        @pl.when(far == 0)
        def _():
            for i, cut in enumerate(cuts(j)):
                if j < PIECES:
                    source = w_in_far.at[rows(W * j + 128 * k + 64 * i, 64, 64), off]
                else:
                    cols = pl.ds(W * (j - PIECES), W)
                    source = w_out_far.at[rows(W * (chip % 2) + 128 * k + 64 * i, 64, 64), cols]
                send(source, blk.at[j, cut, :], w_s.at[0], w_r.at[j, i], up)
                send(source, blk.at[j, cut, :], w_s.at[1], w_r.at[j, i], down)
            pltpu.make_async_copy(whole, blk.at[j], loc.at[j]).start()

    def relay(j, hops):
        last = NT // 2

        @pl.when(far == hops)
        def _():
            for i, cut in enumerate(cuts(j)):
                piece = blk.at[j, cut, :]
                got(piece, w_r.at[j, i])
                if hops < last:
                    send(piece, piece, w_s.at[0], w_r.at[j, i], up)
                send(piece, piece, p_s, p_r.at[j], partner)

        if hops < last:

            @pl.when(far == NT - hops)
            def _():
                for i, cut in enumerate(cuts(j)):
                    piece = blk.at[j, cut, :]
                    got(piece, w_r.at[j, i])
                    if hops < last - 1:
                        send(piece, piece, w_s.at[1], w_r.at[j, i], down)
                    send(piece, piece, p_s, p_r.at[j], partner)

    def relay_end():
        pieces = blk.at[:, half, :]

        @pl.when(far <= 3)
        def _():
            sent(pieces, w_s.at[0])

        @pl.when((far == 0) | (far >= 6))
        def _():
            sent(pieces, w_s.at[1])

        @pl.when(far != 0)
        def _():
            sent(pieces, p_s)

    def layout(j):
        if j < PIECES:
            return j, 3 * W // 16, (p_q, t_q, r2_q, m_q), 0
        return j - PIECES, W // 16, (p_o, t_o, r2_o, m_o), 1

    def axes(j):
        return (x, y) if j % 2 == 0 else (y, x)

    def peer(j, first, i):
        along_x = (j % 2 == 0) == first
        px = (x + i) % SIDE if along_x else x
        py = y if along_x else (y + i) % SIDE
        return ((py * SIDE + px) * 2 + k, t)

    def product(j):
        other = rows(128 * (1 - k), 128, 128)

        @pl.when(far == 0)
        def _():
            pltpu.make_async_copy(blk.at[j], blk.at[j], loc.at[j]).wait()

        @pl.when(far != 0)
        def _():
            got(blk.at[j, other, :], p_r.at[j])

        if j == 0:
            got(wx.at[:, other, :], x_r.at[0])
            for m in range(3):
                wx[m, half, :] = wsc[m, :, mine]
        if j == PIECES:
            got(wxo.at[:, other], x_r.at[1])
            wxo[:, half] = w_ao[mine, :]
        n, part, (p, tt, r2, m_), kind = layout(j)
        if j < PIECES:
            for m in range(3):
                p[n, W * m : W * (m + 1), :] = mm(blk[j], wx[m]).astype(BF16)
        else:
            p[n] = mm(wxo[...], blk[j]).astype(BF16)
        u, v = axes(j)
        if kind:
            for i in range(1, SIDE):
                block = rows(4 * part * ((u + i) % SIDE), 4 * part)
                send(
                    p.at[n, block, :], r1_o.at[n, i - 1],
                    sum_s.at[0, kind], a1_r.at[j], peer(j, True, i),
                )
            return
        for side, way in ((0, 1), (1, SIDE - 1)):
            block = rows(4 * part * ((u + 2) % SIDE) + 2 * part * side, 2 * part)
            send(
                p.at[n, block, :], a1_q.at[n, side],
                sum_s.at[0, kind], a1_r.at[j], peer(j, True, way),
            )

    def turn(j):
        n, part, (p, tt, r2, m_), kind = layout(j)
        u, v = axes(j)
        got(a1_q.at[n], a1_r.at[j])
        for side, way in ((0, 1), (1, SIDE - 1)):
            base = 4 * part * ((u + way) % SIDE)
            cut = rows(base + 2 * part * side, 2 * part)
            p[n, cut, :] = (p[n, cut, :].astype(F32) + a1_q[n, side].astype(F32)).astype(BF16)
            send(
                p.at[n, rows(base, 4 * part), :], b1_q.at[n, side],
                sum_s.at[1, kind], b1_r.at[j], peer(j, True, way),
            )

    def sum1(j):
        n, part, (p, tt, r2, m_), kind = layout(j)
        u, v = axes(j)
        total = p[n, rows(4 * part * u, 4 * part), :].astype(F32)
        if kind:
            got(r1_o.at[n], a1_r.at[j])
            total = total + r1_o[n, 0].astype(F32) + r1_o[n, 1].astype(F32) + r1_o[n, 2].astype(F32)
        else:
            got(b1_q.at[n], b1_r.at[j])
            total = total + b1_q[n, 0].astype(F32) + b1_q[n, 1].astype(F32)
        tt[n] = total.astype(BF16)
        for i in range(1, SIDE):
            to = (v + i) % SIDE
            send(
                tt.at[n, rows(part * to, part), :], r2.at[n, i - 1],
                sum_s.at[2, kind], r2_r.at[j], peer(j, False, i),
            )

    def sum2(j):
        n, part, (p, tt, r2, m_), kind = layout(j)
        u, v = axes(j)
        got(r2.at[n], r2_r.at[j])
        total = tt[n, rows(part * v, part), :].astype(F32)
        for i in range(SIDE - 1):
            total = total + r2[n, i].astype(F32)
        own = rows(part * (4 * u + v), part)
        m_[n, k, own, :] = total.astype(BF16)
        for i in range(1, SIDE):
            send(
                m_.at[n, k, own, :], m_.at[n, k, own, :],
                sum_s.at[3, kind], g1_r.at[j], peer(j, False, i),
            )

    def gather1(j):
        n, part, (p, tt, r2, m_), kind = layout(j)
        u, v = axes(j)
        got(r2.at[n], g1_r.at[j])
        own = rows(4 * part * u, 4 * part)
        for way in range(1, SIDE) if kind else (1, SIDE - 1):
            send(
                m_.at[n, k, own, :], m_.at[n, k, own, :],
                sum_s.at[4, kind], g2_r.at[j], peer(j, True, way),
            )

    def gather2(j):
        n, part, (p, tt, r2, m_), kind = layout(j)
        u, v = axes(j)
        got(b1_q.at[n], g2_r.at[j])
        for side, way in ((0, 1), (1, SIDE - 1)):
            base = 4 * part * ((u + SIDE - way) % SIDE) + 2 * part * side
            block = m_.at[n, k, rows(base, 2 * part), :]
            send(block, block, sum_s.at[5, kind], g3_r.at[j], peer(j, True, way))

    def gather3(j):
        n, part, (p, tt, r2, m_), kind = layout(j)
        if kind:
            got(r1_o.at[n], g2_r.at[j])
        else:
            got(a1_q.at[n], g3_r.at[j])
        send(m_.at[n, k], m_.at[n, k], sum_s.at[6, kind], h_r.at[j], partner)

    begun = []

    def joined(j):
        n, part, (p, tt, r2, m_), kind = layout(j)
        got(m_.at[n, 1 - k], h_r.at[j])
        if j < PIECES:
            piece = ctx[:, W * j : W * (j + 1)]
            for m in range(3):
                for side in range(2):
                    cols = slice(W * side, W * (side + 1))
                    term = mm(piece, m_[n, side, W * m : W * (m + 1), :])
                    if not begun:
                        acc[m, :, cols] = term
                    else:
                        acc[m, :, cols] = acc[m, :, cols] + term
            begun.append(j)

    def sums_end():
        for i, ref in enumerate((a1_q, b1_q, r2_q, r2_q, b1_q, a1_q, m_q.at[:, 0])):
            sent(ref, sum_s.at[i, 0])
        for i, ref in ((0, r1_o), (2, r2_o), (3, r2_o), (4, r1_o), (6, m_o.at[:, 0])):
            sent(ref, sum_s.at[i, 1])

    def pool():
        len_row, len_col, route_row, route_col, end_row, end_col, slot_row, slot_col = tables(
            lengths, route
        )
        values = states[...].astype(F32)
        scale = lax.rsqrt(jnp.mean(values * values, axis=-1, keepdims=True) + EPS)
        normed = values * scale * gain[...].reshape(1, -1)
        high = normed.astype(BF16)
        low = (normed - high.astype(F32)).astype(BF16)
        n = states.shape[0]
        place = iota((lengths.shape[1], n), 1).astype(F32)
        member = onehot((place >= end_col - len_col) & (place < end_col))
        pooled = ((mm(member, high) + mm(member, low)) / len_col).astype(BF16)
        spot = iota((NB * PACK, lengths.shape[1]), 0).astype(F32)
        target = route_row * PACK + slot_row * PIECES
        packed = mm(
            onehot(spot == route_row * PACK + 2 * PIECES + slot_row),
            jnp.ones((lengths.shape[1], W), BF16),
        )
        for j in range(PIECES):
            packed = packed + mm(onehot(spot == target + j), pooled[:, W * j : W * (j + 1)])
        snd[...] = packed.astype(BF16)

    def exchange_start(src, dst, ssem, rsem):
        own = rows(PACK * b, PACK)

        @pl.loop(1, NB)
        def _(i):
            to = (b + i) % NB
            send(src.at[rows(PACK * to, PACK), :], dst.at[own, :], ssem, rsem, (to, t))

        dst[own, :] = src[own, :]

    def exchange_wait(src, dst, ssem, rsem):
        most = pl.ds(0, (NB - 1) * PACK)
        sent(src.at[most, :], ssem)
        got(dst.at[most, :], rsem)

    def slots():
        slot, spot = iota((2 * NB, NB * PACK), 0), iota((2 * NB, NB * PACK), 1)
        base = (slot // 2) * PACK
        arrived = arr[...]
        own = rows(2 * NB * t, 2 * NB)
        for j in range(PIECES):
            pick = onehot(spot == base + (slot % 2) * PIECES + j)
            ctx[own, W * j : W * (j + 1)] = mm(pick, arrived).astype(BF16)
        pick = onehot(spot == base + 2 * PIECES + slot % 2)
        ctx[own, E : E + FLAGS] = mm(pick, arrived[:, :FLAGS]).astype(BF16)

    def ctx_cut(plane, cut):
        plane = (plane + 2 * NT) % NT
        return ctx.at[rows(2 * NB * plane + NB * cut, NB), :]

    def ctx_send(step, cut):
        for side, sign, dev in ((0, -1, up), (1, 1, down)):
            if step < 3 or side == cut:
                block = ctx_cut(t + sign * step, cut)
                send(block, block, c_s.at[side], c_r.at[side, step, cut], dev)

    def ctx_step(step, cut):
        for side, sign in ((0, -1), (1, 1)):
            if step < 3 or side == cut:
                got(ctx_cut(t + sign * (step + 1), cut), c_r.at[side, step, cut])
        if step < 3:
            ctx_send(step + 1, cut)

    def ctx_end():
        for side in range(2):
            sent(ctx.at[pl.ds(0, 7 * NB), :], c_s.at[side])

    def latents():
        load_wait("in")
        part = mm(ctx[:, :E], w_in[...]).astype(BF16)
        lat[...] = part
        wide = part.astype(F32)
        squares = wide * wide
        high = squares.astype(BF16)
        low = (squares - high.astype(F32)).astype(BF16)
        ones = jnp.ones((8, part.shape[1]), BF16)
        sqs[t] = mm_t(ones, high) + mm_t(ones, low)

        @pl.loop(1, NT)
        def _(i):
            send(sqs.at[t], sqs.at[t], q_s, q_r, (b, (t + i) % NT))

    def scales():
        most = sqs.at[pl.ds(0, NT - 1)]
        sent(most, q_s)
        got(most, q_r)
        total = sqs[0]
        for i in range(1, NT):
            total = total + sqs[i]
        scale = lax.rsqrt(total / D + EPS)
        return jnp.transpose(scale)[:, 0:1]

    def project():
        scale = scales()
        for m in range(2):
            qk[m] = (acc[m] * scale).astype(BF16)
        values = (acc[2] * scale).astype(BF16)
        for h in range(values.shape[1] // DH):
            vals[:, 2 * DH * h : 2 * DH * h + DH] = values[:, DH * h : DH * (h + 1)]

    def mask():
        for h in range(vals.shape[1] // (2 * DH)):
            vals[:, 2 * DH * h + DH : 2 * DH * (h + 1)] = jnp.ones((CTX, DH), BF16)
        seen = mm_t(jnp.ones((8, FLAGS), BF16), ctx[:, E : E + FLAGS])[0:1, :] > 0.5
        line, place = iota((CTX, CTX), 0), iota((CTX, CTX), 1)
        allowed = ((place < line) & seen) | (place == line)
        bias[...] = jnp.where(allowed, 0.0, -1e30)

    def head(h):
        cols = slice(DH * h, DH * (h + 1))
        for i in range(CTX // 128):
            lines = slice(128 * i, 128 * (i + 1))
            n = 128 * (i + 1)
            scores = mm_t(qk[0, lines, cols], qk[1, :n, cols])
            scores = scores * (DH ** (-0.5) * LOG2E) + bias[lines, :n]
            raised = jnp.exp2(scores - jnp.max(scores, axis=-1, keepdims=True)).astype(BF16)
            mixed = mm(raised, vals[:n, 2 * DH * h : 2 * DH * (h + 1)])
            att[lines, cols] = (mixed[:, :DH] / mixed[:, DH:]).astype(BF16)

    def z_rows(plane, start, size):
        plane = (plane + 2 * NT) % NT
        return rows(2 * NB * plane + start, size)

    def z_first(n):
        value = mm(att[:, :W], m_o[n, 0]) + mm(att[:, W:], m_o[n, 1])
        zp[n] = (value + lw[:, W * n : W * (n + 1)]).astype(BF16)
        for side, dev in ((0, up), (1, down)):
            send(
                zp.at[n, z_rows(t + 4, NB * side, NB), :], zr.at[n, 0, side, pl.ds(0, NB), :],
                z_s.at[0], z_r.at[n, 0], dev,
            )

    def z_add(n, step):
        if step == 1:
            got(zr.at[n, 0, :, pl.ds(0, NB), :], z_r.at[n, 0])
        else:
            got(zr.at[n, step - 1], z_r.at[n, step - 1])
        for side, sign, dev in ((0, 1, up), (1, -1, down)):
            plane = t + sign * (4 - step)
            if step == 1:
                place, came = z_rows(plane, NB * side, NB), zr[n, 0, side, 0:NB, :]
            else:
                place, came = z_rows(plane, 0, 2 * NB), zr[n, step - 1, side]
            zp[n, place, :] = (zp[n, place, :].astype(F32) + came.astype(F32)).astype(BF16)
            send(
                zp.at[n, z_rows(plane, 0, 2 * NB), :], zr.at[n, step, side],
                z_s.at[1], z_r.at[n, step], dev,
            )

    packed = []

    def z_last(n):
        got(zr.at[n, 3], z_r.at[n, 3])
        total = zp[n, z_rows(t, 0, 2 * NB), :].astype(F32)
        total = total + zr[n, 3, 0].astype(F32) + zr[n, 3, 1].astype(F32)
        spot, slot = iota((NB * PACK, 2 * NB), 0), iota((NB * PACK, 2 * NB), 1)
        pick = onehot(spot == (slot // 2) * PACK + (slot % 2) * PIECES + n)
        term = mm(pick, total.astype(BF16))
        packf[...] = packf[...] + term if packed else term
        packed.append(n)

    def z_end():
        sent(zr.at[:, 0, :, pl.ds(0, NB), :], z_s.at[0])
        sent(zr.at[:, pl.ds(1, 3)], z_s.at[1])

    def decode():
        len_row, len_col, route_row, route_col, end_row, end_col, slot_row, slot_col = tables(
            lengths, route
        )
        n, patches = states.shape[0], lengths.shape[1]
        place = iota((n, patches), 0).astype(F32)
        member = onehot((place >= end_row - len_row) & (place < end_row))
        spot = iota((patches, NB * PACK), 1).astype(F32)
        target = route_col * PACK + slot_col * PIECES
        picks = jnp.concatenate([onehot(spot == target + j) for j in range(PIECES)], axis=0)
        values = mm(picks, arr2[...]).astype(BF16)
        total = jnp.zeros((patches, w_head.shape[1]), F32)
        for j in range(PIECES):
            total = total + mm(values[patches * j : patches * (j + 1), :], w_head[W * j : W * (j + 1), :])
        high = total.astype(BF16)
        low = (total - high.astype(F32)).astype(BF16)
        out[...] = (base[...] + mm(member, high) + mm(member, low)).astype(BF16)

    def own_logits():
        load_wait("head")
        base[...] = mm(states[...], w_head[...])

    def add_residual():
        load_wait("out")
        lw[...] = mm(lat[...], w_out[...])

    def exch():
        exchange_wait(snd, arr, a_s, a_r)
        slots()

    def ctx_go():
        ctx_send(0, 0)
        ctx_send(0, 1)

    def finish():
        sent(wsc.at[:, :, theirs], x_s.at[0])
        sent(wxo.at[:, half], x_s.at[1])
        relay_end()
        ctx_end()
        sums_end()
        z_end()

    stages = {
        "start": start, "relay": relay, "product": product, "turn": turn, "sum1": sum1,
        "sum2": sum2, "gather1": gather1, "gather2": gather2, "gather3": gather3,
        "joined": joined, "exch": exch, "ctxgo": ctx_go, "ctx": ctx_step, "lat": latents, "res": add_residual, "mask": mask, "own": own_logits,
        "proj": project, "head": head, "zf": z_first, "za": z_add, "zl": z_last,
    }
    load_start()
    greet()
    load_wait("gain", "scale", "lengths", "route", "states")
    pool()
    load_wait("q", "k", "v", "ao")
    scale_weights()
    meet()
    swap_weights()
    start(0)
    start(1)
    exchange_start(snd, arr, a_s, a_r)
    for name, *where in ORDER:
        stages[name](*where)
    snd2[...] = packf[...].astype(BF16)
    exchange_start(snd2, arr2, b_s, b_r)
    exchange_wait(snd2, arr2, b_s, b_r)
    decode()
    finish()


def body(
    byte_states, enc_gain, patch_lengths, patch_route, w_in, latent_gain,
    w_query, w_key, w_value, w_attn_out, w_out, w_head,
):
    vmem = pl.BlockSpec(memory_space=pltpu.VMEM)
    far = pl.BlockSpec(memory_space=pl.ANY)
    dma = pltpu.SemaphoreType.DMA
    part_q, part_o = 3 * W // 16, W // 16

    def buf(*shape, dtype=BF16):
        return pltpu.VMEM(shape, dtype)

    inputs = (
        byte_states, enc_gain, patch_lengths, patch_route.reshape(1, -1), w_in,
        latent_gain.reshape(NB, -1), w_query, w_key, w_value, w_attn_out, w_out, w_head,
    )
    scratch = [
        *[buf(*value.shape, dtype=value.dtype) for value in inputs],
        dma((len(inputs),)),
        buf(STAGES, W, W),
        buf(3, 128, 2 * W),
        buf(3, W, W),
        buf(W, W),
        buf(PIECES, 3 * W, W),
        buf(PIECES, W, W),
        buf(PIECES, 2, 2 * part_q, W),
        buf(PIECES, 2, 4 * part_q, W),
        buf(PIECES, 3, 4 * part_o, W),
        buf(PIECES, 4 * part_q, W),
        buf(PIECES, 4 * part_o, W),
        buf(PIECES, 3, part_q, W),
        buf(PIECES, 3, part_o, W),
        buf(PIECES, 2, 3 * W, W),
        buf(PIECES, 2, W, W),
        buf(NB * PACK, W),
        buf(NB * PACK, W),
        buf(NB * PACK, W),
        buf(NB * PACK, W),
        buf(CTX, E + FLAGS),
        buf(CTX, 2 * W),
        buf(NT, 8, CTX, dtype=F32),
        buf(3, CTX, 2 * W, dtype=F32),
        buf(2, CTX, 2 * W),
        buf(CTX, 4 * W),
        buf(CTX, CTX, dtype=F32),
        buf(byte_states.shape[0], w_head.shape[1], dtype=F32),
        buf(CTX, 2 * W),
        buf(CTX, E, dtype=F32),
        buf(PIECES, CTX, W),
        buf(PIECES, 4, 2, 2 * NB, W),
        buf(NB * PACK, W, dtype=F32),
        dma((2,)), dma((STAGES, 2)), dma, dma((STAGES,)), dma((STAGES,)),
        dma((2,)), dma((2,)), dma, dma, dma((2,)), dma((2, 4, 2)), dma, dma,
        dma((7, 2)),
        dma((STAGES,)), dma((PIECES,)), dma((STAGES,)), dma((STAGES,)), dma((STAGES,)),
        dma((PIECES,)), dma((STAGES,)),
        dma((2,)), dma((PIECES, 4)), dma, dma,
    ]
    return pl.pallas_call(
        kernel,
        out_shape=jax.ShapeDtypeStruct((byte_states.shape[0], w_head.shape[1]), BF16),
        in_specs=[far] * 12,
        out_specs=vmem,
        scratch_shapes=scratch,
        compiler_params=pltpu.CompilerParams(
            collective_id=0, has_side_effects=True, vmem_limit_bytes=56 * 1024 * 1024
        ),
    )(
        *inputs
    )


def solution(mesh):
    return jax.shard_map(
        body,
        mesh=mesh,
        in_specs=(
            P(("byte", "tensor"), None),
            P(),
            P(("byte", "tensor"), None),
            P(("byte", "tensor"), None, None),
            P(None, "tensor"),
            P(),
            P("byte", "tensor"),
            P("byte", "tensor"),
            P("byte", "tensor"),
            P("tensor", "byte"),
            P("tensor", None),
            P(),
        ),
        out_specs=P(("byte", "tensor"), None),
        check_vma=False,
    )
```

```python
import jax
import jax.numpy as jnp
from jax import lax
from jax.experimental import pallas as pl
from jax.experimental.pallas import tpu as pltpu
from jax.sharding import PartitionSpec as P

MESH = pl.DeviceIdType.MESH
BF16 = jnp.bfloat16
F32 = jnp.float32
DH = 128
EPS = 1e-06
LOG2E = 1.4426950408889634
SIDE = 4
NB = 32
NT = 8
E = 1280
D = 4096
CTX = 512
W = 256
PIECES = E // W
STAGES = 2 * PIECES
FLAGS = 128
PACK = 16

(
    START, RELAY, PRODUCT, TURN, SUM1, SUM2, GATHER1, GATHER2, GATHER3, JOINED, EXCH,
    CTXGO, RING, LAT, RES, MASK, OWN, PROJ, HEAD, ZF, ZA, ZL,
) = range(22)
ORDER = (
    (START, 2), (START, 3), (START, 4), (RELAY, 0, 1), (RELAY, 1, 1), (RELAY, 0, 2), (RELAY, 2, 1),
    (RELAY, 1, 2), (EXCH,), (RELAY, 3, 1), (RELAY, 0, 3), (START, 5), (RELAY, 2, 2), (RELAY, 4, 1),
    (RELAY, 1, 3), (START, 6), (RELAY, 3, 2), (RELAY, 0, 4), (RELAY, 5, 1), (RELAY, 2, 3),
    (START, 7), (RELAY, 4, 2), (PRODUCT, 0), (RELAY, 1, 4), (RELAY, 6, 1), (RELAY, 3, 3),
    (START, 8), (PRODUCT, 1), (RELAY, 5, 2), (RELAY, 2, 4), (RELAY, 7, 1), (RELAY, 4, 3),
    (PRODUCT, 2), (START, 9), (RELAY, 6, 2), (RELAY, 3, 4), (TURN, 0), (RELAY, 8, 1), (RELAY, 5, 3),
    (PRODUCT, 3), (RELAY, 7, 2), (RELAY, 4, 4), (TURN, 1), (RELAY, 9, 1), (RELAY, 6, 3),
    (PRODUCT, 4), (RELAY, 8, 2), (TURN, 2), (RELAY, 5, 4), (RELAY, 7, 3), (RELAY, 9, 2), (TURN, 3),
    (RELAY, 6, 4), (PRODUCT, 5), (SUM1, 0), (RELAY, 8, 3), (TURN, 4), (RELAY, 7, 4), (PRODUCT, 6),
    (SUM1, 1), (RELAY, 9, 3), (CTXGO,), (RELAY, 8, 4), (PRODUCT, 7), (SUM1, 2), (SUM1, 3),
    (RELAY, 9, 4), (PRODUCT, 8), (SUM1, 5), (RING, 0, 0), (SUM1, 4), (PRODUCT, 9), (SUM2, 0),
    (SUM1, 6), (RING, 0, 1), (SUM1, 7), (SUM2, 1), (OWN,), (SUM2, 2), (SUM2, 3), (RING, 1, 0),
    (SUM2, 4), (SUM1, 8), (SUM2, 5), (SUM2, 7), (RING, 1, 1), (SUM1, 9), (GATHER1, 1), (GATHER1, 0),
    (SUM2, 6), (GATHER1, 3), (GATHER1, 5), (RING, 2, 0), (GATHER1, 2), (GATHER1, 7), (GATHER1, 4),
    (SUM2, 8), (SUM2, 9), (RING, 2, 1), (RING, 3, 0), (GATHER2, 1), (GATHER2, 0), (GATHER1, 6),
    (RING, 3, 1), (GATHER2, 2), (GATHER2, 3), (LAT,), (MASK,), (GATHER3, 5), (GATHER2, 4),
    (GATHER1, 9), (GATHER3, 7), (GATHER1, 8), (GATHER3, 0), (JOINED, 5), (JOINED, 7), (GATHER3, 1),
    (RES,), (GATHER3, 6), (GATHER3, 3), (JOINED, 0), (GATHER3, 2), (JOINED, 1), (GATHER3, 9),
    (GATHER3, 4), (JOINED, 6), (JOINED, 3), (GATHER3, 8), (JOINED, 2), (JOINED, 9), (JOINED, 4),
    (JOINED, 8), (PROJ,), (HEAD, 0), (ZF, 0), (ZF, 1), (ZF, 2), (ZF, 3), (ZF, 4), (HEAD, 1),
    (ZA, 0, 1), (ZA, 1, 1), (ZA, 2, 1), (ZA, 3, 1), (ZA, 4, 1), (HEAD, 2), (ZA, 0, 2), (ZA, 1, 2),
    (ZA, 2, 2), (ZA, 3, 2), (ZA, 4, 2), (HEAD, 3), (ZA, 0, 3), (ZA, 1, 3), (ZA, 2, 3), (ZA, 3, 3),
    (ZA, 4, 3), (HEAD, 4), (ZL, 0), (ZL, 1), (ZL, 2), (ZL, 3), (ZL, 4),
)


def mm(a, b):
    return jnp.dot(a, b, preferred_element_type=F32)


def mm_t(a, b):
    return lax.dot_general(a, b, (((1,), (1,)), ((), ())), preferred_element_type=F32)


def iota(shape, dim):
    return lax.broadcasted_iota(jnp.int32, shape, dim)


def onehot(mask):
    return jnp.where(mask, 1.0, 0.0).astype(BF16)


def tables(lengths, route):
    n = lengths.shape[1]
    down, across = iota((n, n), 0), iota((n, n), 1)
    eye = down == across

    def column(row):
        return jnp.sum(jnp.where(eye, row, 0.0), axis=1, keepdims=True)

    len_row = lengths[...].astype(F32)
    route_row = route[...].astype(F32)
    len_col, route_col = column(len_row), column(route_row)
    end_row = jnp.sum(jnp.where(down <= across, len_col, 0.0), axis=0, keepdims=True)
    end_col = jnp.sum(jnp.where(across <= down, len_row, 0.0), axis=1, keepdims=True)
    same = jnp.where(route_row == route_col, 1.0, 0.0)
    slot_row = jnp.sum(jnp.where(down < across, same, 0.0), axis=0, keepdims=True)
    slot_col = jnp.sum(jnp.where(across < down, same, 0.0), axis=1, keepdims=True)
    return len_row, len_col, route_row, route_col, end_row, end_col, slot_row, slot_col


def kernel(
    states_far, gain_far, lengths_far, route_far, w_in_far, lat_gain_far,
    w_q_far, w_k_far, w_v_far, w_ao_far, w_out_far, w_head_far, out,
    states, gain, lengths, route, w_in, lat_gain, w_q, w_k, w_v, w_ao, w_out, w_head, in_s,
    blk, wsc, wx, wxo, p_q, p_o, a1_q, b1_q, r1_o, t_q, t_o, r2_q, r2_o, m_q, m_o,
    snd, arr, snd2, arr2, ctx, lat, sqs, acc, qk, vals, bias, base, att, lw, zp, zr, packf,
    w_s, w_r, p_s, p_r, loc, x_s, x_r, a_s, a_r, c_s, c_r, q_s, q_r,
    sum_s, a1_r, b1_r, r2_r, g1_r, g2_r, g3_r, h_r, z_s, z_r, b_s, b_r,
):
    b = lax.axis_index("byte")
    t = lax.axis_index("tensor")
    k = b % 2
    chip = b // 2
    x = chip % SIDE
    y = chip // SIDE
    far = (t - chip // 2 + NT) % NT
    up = (b, (t + 1) % NT)
    down = (b, (t + NT - 1) % NT)
    partner = (b + 1 - 2 * k, t)

    def rcopy(src, dst, ssem, rsem, dev):
        return pltpu.make_async_remote_copy(
            src_ref=src, dst_ref=dst, send_sem=ssem, recv_sem=rsem, device_id=dev, device_id_type=MESH
        )

    def send(src, dst, ssem, rsem, dev):
        rcopy(src, dst, ssem, rsem, dev).start()

    def got(dst, rsem):
        rcopy(dst, dst, rsem, rsem, partner).wait_recv()

    def sent(src, ssem):
        rcopy(src, src, ssem, ssem, partner).wait_send()

    def rows(start, size, step=16):
        return pl.ds(pl.multiple_of(start, step), size)

    bar = pltpu.get_barrier_semaphore()
    half = rows(128 * k, 128, 128)
    mine = rows(W * k, W, W)
    theirs = rows(W * (1 - k), W, W)

    def greet():
        @pl.loop(1, NB)
        def _(i):
            pl.semaphore_signal(bar, inc=1, device_id=((b + i) % NB, t), device_id_type=MESH)

        @pl.loop(1, NT)
        def _(i):
            pl.semaphore_signal(bar, inc=1, device_id=(b, (t + i) % NT), device_id_type=MESH)

    def scale_weights():
        g_row = lat_gain[pl.ds(b, 1), :]
        eye = iota((128, 128), 0) == iota((128, 128), 1)
        g_col = jnp.sum(jnp.where(eye, g_row, 0.0), axis=1, keepdims=True)
        for m, weight in enumerate((w_q, w_k, w_v)):
            wsc[m] = (weight[...].astype(F32) * g_col).astype(BF16)

    loads = {
        "gain": (lat_gain_far, lat_gain), "scale": (gain_far, gain), "lengths": (lengths_far, lengths),
        "route": (route_far, route), "states": (states_far, states), "q": (w_q_far, w_q),
        "k": (w_k_far, w_k), "v": (w_v_far, w_v), "ao": (w_ao_far, w_ao), "in": (w_in_far, w_in),
        "out": (w_out_far, w_out), "head": (w_head_far, w_head),
    }
    places = {name: i for i, name in enumerate(loads)}

    def load_start():
        for name, (src, dst) in loads.items():
            pltpu.make_async_copy(src, dst, in_s.at[places[name]]).start()

    def load_wait(*names):
        for name in names:
            src, dst = loads[name]
            pltpu.make_async_copy(src, dst, in_s.at[places[name]]).wait()

    def meet():
        pl.semaphore_wait(bar, NB + NT - 2)

    def swap_weights():
        for m in range(3):
            send(wsc.at[m, :, theirs], wx.at[m, half, :], x_s.at[0], x_r.at[0], partner)
        send(w_ao.at[theirs, :], wxo.at[:, half], x_s.at[1], x_r.at[1], partner)

    off = rows(W * (chip % 2), W, W)

    def cuts(j):
        return [rows(128 * k + 64 * i, 64, 64) for i in range(2)]

    def start(j):
        if j < PIECES:
            whole = w_in_far.at[pl.ds(W * j, W), off]
        else:
            whole = w_out_far.at[off, pl.ds(W * (j - PIECES), W)]

        @pl.when(far == 0)
        def _():
            for i, cut in enumerate(cuts(j)):
                if j < PIECES:
                    source = w_in_far.at[rows(W * j + 128 * k + 64 * i, 64, 64), off]
                else:
                    cols = pl.ds(W * (j - PIECES), W)
                    source = w_out_far.at[rows(W * (chip % 2) + 128 * k + 64 * i, 64, 64), cols]
                send(source, blk.at[j, cut, :], w_s.at[0], w_r.at[j, i], up)
                send(source, blk.at[j, cut, :], w_s.at[1], w_r.at[j, i], down)
            pltpu.make_async_copy(whole, blk.at[j], loc.at[j]).start()

    def relay(j, hops):
        last = NT // 2

        @pl.when(far == hops)
        def _():
            for i, cut in enumerate(cuts(j)):
                piece = blk.at[j, cut, :]
                got(piece, w_r.at[j, i])
                if hops < last:
                    send(piece, piece, w_s.at[0], w_r.at[j, i], up)
                send(piece, piece, p_s, p_r.at[j], partner)

        if hops < last:

            @pl.when(far == NT - hops)
            def _():
                for i, cut in enumerate(cuts(j)):
                    piece = blk.at[j, cut, :]
                    got(piece, w_r.at[j, i])
                    if hops < last - 1:
                        send(piece, piece, w_s.at[1], w_r.at[j, i], down)
                    send(piece, piece, p_s, p_r.at[j], partner)

    def relay_end():
        pieces = blk.at[:, half, :]

        @pl.when(far <= 3)
        def _():
            sent(pieces, w_s.at[0])

        @pl.when((far == 0) | (far >= 6))
        def _():
            sent(pieces, w_s.at[1])

        @pl.when(far != 0)
        def _():
            sent(pieces, p_s)

    def layout(j):
        if j < PIECES:
            return j, 3 * W // 16, (p_q, t_q, r2_q, m_q), 0
        return j - PIECES, W // 16, (p_o, t_o, r2_o, m_o), 1

    def axes(j):
        return (x, y) if j % 2 == 0 else (y, x)

    def peer(j, first, i):
        along_x = (j % 2 == 0) == first
        px = (x + i) % SIDE if along_x else x
        py = y if along_x else (y + i) % SIDE
        return ((py * SIDE + px) * 2 + k, t)

    def product(j):
        other = rows(128 * (1 - k), 128, 128)

        @pl.when(far == 0)
        def _():
            pltpu.make_async_copy(blk.at[j], blk.at[j], loc.at[j]).wait()

        @pl.when(far != 0)
        def _():
            got(blk.at[j, other, :], p_r.at[j])

        if j == 0:
            got(wx.at[:, other, :], x_r.at[0])
            for m in range(3):
                wx[m, half, :] = wsc[m, :, mine]
        if j == PIECES:
            got(wxo.at[:, other], x_r.at[1])
            wxo[:, half] = w_ao[mine, :]
        n, part, (p, tt, r2, m_), kind = layout(j)
        if j < PIECES:
            for m in range(3):
                p[n, W * m : W * (m + 1), :] = mm(blk[j], wx[m]).astype(BF16)
        else:
            p[n] = mm(wxo[...], blk[j]).astype(BF16)
        u, v = axes(j)
        if kind:
            for i in range(1, SIDE):
                block = rows(4 * part * ((u + i) % SIDE), 4 * part)
                send(
                    p.at[n, block, :], r1_o.at[n, i - 1],
                    sum_s.at[0, kind], a1_r.at[j], peer(j, True, i),
                )
            return
        for side, way in ((0, 1), (1, SIDE - 1)):
            block = rows(4 * part * ((u + 2) % SIDE) + 2 * part * side, 2 * part)
            send(
                p.at[n, block, :], a1_q.at[n, side],
                sum_s.at[0, kind], a1_r.at[j], peer(j, True, way),
            )

    def turn(j):
        n, part, (p, tt, r2, m_), kind = layout(j)
        u, v = axes(j)
        got(a1_q.at[n], a1_r.at[j])
        for side, way in ((0, 1), (1, SIDE - 1)):
            base = 4 * part * ((u + way) % SIDE)
            cut = rows(base + 2 * part * side, 2 * part)
            p[n, cut, :] = (p[n, cut, :].astype(F32) + a1_q[n, side].astype(F32)).astype(BF16)
            send(
                p.at[n, rows(base, 4 * part), :], b1_q.at[n, side],
                sum_s.at[1, kind], b1_r.at[j], peer(j, True, way),
            )

    def sum1(j):
        n, part, (p, tt, r2, m_), kind = layout(j)
        u, v = axes(j)
        total = p[n, rows(4 * part * u, 4 * part), :].astype(F32)
        if kind:
            got(r1_o.at[n], a1_r.at[j])
            total = total + r1_o[n, 0].astype(F32) + r1_o[n, 1].astype(F32) + r1_o[n, 2].astype(F32)
        else:
            got(b1_q.at[n], b1_r.at[j])
            total = total + b1_q[n, 0].astype(F32) + b1_q[n, 1].astype(F32)
        tt[n] = total.astype(BF16)
        for i in range(1, SIDE):
            to = (v + i) % SIDE
            send(
                tt.at[n, rows(part * to, part), :], r2.at[n, i - 1],
                sum_s.at[2, kind], r2_r.at[j], peer(j, False, i),
            )

    def sum2(j):
        n, part, (p, tt, r2, m_), kind = layout(j)
        u, v = axes(j)
        got(r2.at[n], r2_r.at[j])
        total = tt[n, rows(part * v, part), :].astype(F32)
        for i in range(SIDE - 1):
            total = total + r2[n, i].astype(F32)
        own = rows(part * (4 * u + v), part)
        m_[n, k, own, :] = total.astype(BF16)
        for i in range(1, SIDE):
            send(
                m_.at[n, k, own, :], m_.at[n, k, own, :],
                sum_s.at[3, kind], g1_r.at[j], peer(j, False, i),
            )

    def gather1(j):
        n, part, (p, tt, r2, m_), kind = layout(j)
        u, v = axes(j)
        got(r2.at[n], g1_r.at[j])
        own = rows(4 * part * u, 4 * part)
        for way in range(1, SIDE) if kind else (1, SIDE - 1):
            send(
                m_.at[n, k, own, :], m_.at[n, k, own, :],
                sum_s.at[4, kind], g2_r.at[j], peer(j, True, way),
            )

    def gather2(j):
        n, part, (p, tt, r2, m_), kind = layout(j)
        u, v = axes(j)
        got(b1_q.at[n], g2_r.at[j])
        for side, way in ((0, 1), (1, SIDE - 1)):
            base = 4 * part * ((u + SIDE - way) % SIDE) + 2 * part * side
            block = m_.at[n, k, rows(base, 2 * part), :]
            send(block, block, sum_s.at[5, kind], g3_r.at[j], peer(j, True, way))

    def gather3(j):
        n, part, (p, tt, r2, m_), kind = layout(j)
        if kind:
            got(r1_o.at[n], g2_r.at[j])
        else:
            got(a1_q.at[n], g3_r.at[j])
        send(m_.at[n, k], m_.at[n, k], sum_s.at[6, kind], h_r.at[j], partner)

    begun = []

    def joined(j):
        n, part, (p, tt, r2, m_), kind = layout(j)
        got(m_.at[n, 1 - k], h_r.at[j])
        if j < PIECES:
            piece = ctx[:, W * j : W * (j + 1)]
            for m in range(3):
                for side in range(2):
                    cols = slice(W * side, W * (side + 1))
                    term = mm(piece, m_[n, side, W * m : W * (m + 1), :])
                    if not begun:
                        acc[m, :, cols] = term
                    else:
                        acc[m, :, cols] = acc[m, :, cols] + term
            begun.append(j)

    def sums_end():
        for i, ref in enumerate((a1_q, b1_q, r2_q, r2_q, b1_q, a1_q, m_q.at[:, 0])):
            sent(ref, sum_s.at[i, 0])
        for i, ref in ((0, r1_o), (2, r2_o), (3, r2_o), (4, r1_o), (6, m_o.at[:, 0])):
            sent(ref, sum_s.at[i, 1])

    def pool():
        len_row, len_col, route_row, route_col, end_row, end_col, slot_row, slot_col = tables(
            lengths, route
        )
        values = states[...].astype(F32)
        scale = lax.rsqrt(jnp.mean(values * values, axis=-1, keepdims=True) + EPS)
        normed = values * scale * gain[...].reshape(1, -1)
        high = normed.astype(BF16)
        low = (normed - high.astype(F32)).astype(BF16)
        n = states.shape[0]
        place = iota((lengths.shape[1], n), 1).astype(F32)
        member = onehot((place >= end_col - len_col) & (place < end_col))
        pooled = ((mm(member, high) + mm(member, low)) / len_col).astype(BF16)
        spot = iota((NB * PACK, lengths.shape[1]), 0).astype(F32)
        target = route_row * PACK + slot_row * PIECES
        packed = mm(
            onehot(spot == route_row * PACK + 2 * PIECES + slot_row),
            jnp.ones((lengths.shape[1], W), BF16),
        )
        for j in range(PIECES):
            packed = packed + mm(onehot(spot == target + j), pooled[:, W * j : W * (j + 1)])
        snd[...] = packed.astype(BF16)

    def exchange_start(src, dst, ssem, rsem):
        own = rows(PACK * b, PACK)

        @pl.loop(1, NB)
        def _(i):
            to = (b + i) % NB
            send(src.at[rows(PACK * to, PACK), :], dst.at[own, :], ssem, rsem, (to, t))

        dst[own, :] = src[own, :]

    def exchange_wait(src, dst, ssem, rsem):
        most = pl.ds(0, (NB - 1) * PACK)
        sent(src.at[most, :], ssem)
        got(dst.at[most, :], rsem)

    def slots():
        slot, spot = iota((2 * NB, NB * PACK), 0), iota((2 * NB, NB * PACK), 1)
        base = (slot // 2) * PACK
        arrived = arr[...]
        own = rows(2 * NB * t, 2 * NB)
        for j in range(PIECES):
            pick = onehot(spot == base + (slot % 2) * PIECES + j)
            ctx[own, W * j : W * (j + 1)] = mm(pick, arrived).astype(BF16)
        pick = onehot(spot == base + 2 * PIECES + slot % 2)
        ctx[own, E : E + FLAGS] = mm(pick, arrived[:, :FLAGS]).astype(BF16)

    def ctx_cut(plane, cut):
        plane = (plane + 2 * NT) % NT
        return ctx.at[rows(2 * NB * plane + NB * cut, NB), :]

    def ctx_send(step, cut):
        for side, sign, dev in ((0, -1, up), (1, 1, down)):
            if step < 3 or side == cut:
                block = ctx_cut(t + sign * step, cut)
                send(block, block, c_s.at[side], c_r.at[side, step, cut], dev)

    def ctx_step(step, cut):
        for side, sign in ((0, -1), (1, 1)):
            if step < 3 or side == cut:
                got(ctx_cut(t + sign * (step + 1), cut), c_r.at[side, step, cut])
        if step < 3:
            ctx_send(step + 1, cut)

    def ctx_end():
        for side in range(2):
            sent(ctx.at[pl.ds(0, 7 * NB), :], c_s.at[side])

    def latents():
        load_wait("in")
        part = mm(ctx[:, :E], w_in[...]).astype(BF16)
        lat[...] = part
        wide = part.astype(F32)
        squares = wide * wide
        high = squares.astype(BF16)
        low = (squares - high.astype(F32)).astype(BF16)
        ones = jnp.ones((8, part.shape[1]), BF16)
        sqs[t] = mm_t(ones, high) + mm_t(ones, low)

        @pl.loop(1, NT)
        def _(i):
            send(sqs.at[t], sqs.at[t], q_s, q_r, (b, (t + i) % NT))

    def scales():
        most = sqs.at[pl.ds(0, NT - 1)]
        sent(most, q_s)
        got(most, q_r)
        total = sqs[0]
        for i in range(1, NT):
            total = total + sqs[i]
        scale = lax.rsqrt(total / D + EPS)
        return jnp.transpose(scale)[:, 0:1]

    def project():
        scale = scales()
        for m in range(2):
            qk[m] = (acc[m] * scale).astype(BF16)
        values = (acc[2] * scale).astype(BF16)
        for h in range(values.shape[1] // DH):
            vals[:, 2 * DH * h : 2 * DH * h + DH] = values[:, DH * h : DH * (h + 1)]

    def mask():
        for h in range(vals.shape[1] // (2 * DH)):
            vals[:, 2 * DH * h + DH : 2 * DH * (h + 1)] = jnp.ones((CTX, DH), BF16)
        seen = mm_t(jnp.ones((8, FLAGS), BF16), ctx[:, E : E + FLAGS])[0:1, :] > 0.5
        line, place = iota((CTX, CTX), 0), iota((CTX, CTX), 1)
        allowed = ((place < line) & seen) | (place == line)
        bias[...] = jnp.where(allowed, 0.0, -1e30)

    def planes(step):
        return (t + 4,) if step == 0 else (t,) if step == 4 else (t + 4 - step, t - 4 + step)

    def head(step):
        lines = [z_rows(plane, 0, 2 * NB) for plane in planes(step)]
        size = 2 * NB * len(lines)
        asks = jnp.concatenate([qk[0, line, :] for line in lines], axis=0)
        hide = jnp.concatenate([bias[line, :] for line in lines], axis=0)
        for h in range(asks.shape[1] // DH):
            cols = slice(DH * h, DH * (h + 1))
            scores = mm_t(asks[:, cols], qk[1, :, cols]) * (DH ** (-0.5) * LOG2E) + hide
            raised = jnp.exp2(scores - jnp.max(scores, axis=-1, keepdims=True)).astype(BF16)
            mixed = mm(raised, vals[:, 2 * DH * h : 2 * DH * (h + 1)])
            att[0:size, cols] = (mixed[:, :DH] / mixed[:, DH:]).astype(BF16)

    def outputs(n, step):
        lines = [z_rows(plane, 0, 2 * NB) for plane in planes(step)]
        size = 2 * NB * len(lines)
        value = mm(att[0:size, :W], m_o[n, 0]) + mm(att[0:size, W:], m_o[n, 1])
        cols = slice(W * n, W * (n + 1))
        return [
            value[2 * NB * i : 2 * NB * (i + 1), :] + lw[line, cols] for i, line in enumerate(lines)
        ]

    def z_rows(plane, start, size):
        plane = (plane + 2 * NT) % NT
        return rows(2 * NB * plane + start, size)

    def z_first(n):
        zp[n, z_rows(t + 4, 0, 2 * NB), :] = outputs(n, 0)[0].astype(BF16)
        for side, dev in ((0, up), (1, down)):
            send(
                zp.at[n, z_rows(t + 4, NB * side, NB), :], zr.at[n, 0, side, pl.ds(0, NB), :],
                z_s.at[0], z_r.at[n, 0], dev,
            )

    def z_add(n, step):
        values = outputs(n, step)
        if step == 1:
            got(zr.at[n, 0, :, pl.ds(0, NB), :], z_r.at[n, 0])
        else:
            got(zr.at[n, step - 1], z_r.at[n, step - 1])
        for side, sign, dev in ((0, 1, up), (1, -1, down)):
            value = values[side]
            place = z_rows(t + sign * (4 - step), 0, 2 * NB)
            if step == 1:
                came = zr[n, 0, side, 0:NB, :].astype(F32)
                whole = [value[:NB, :], value[NB:, :]]
                whole[side] = whole[side] + came
                value = jnp.concatenate(whole, axis=0)
            else:
                value = value + zr[n, step - 1, side].astype(F32)
            zp[n, place, :] = value.astype(BF16)
            send(zp.at[n, place, :], zr.at[n, step, side], z_s.at[1], z_r.at[n, step], dev)

    packed = []

    def z_last(n):
        total = outputs(n, 4)[0]
        got(zr.at[n, 3], z_r.at[n, 3])
        total = total + zr[n, 3, 0].astype(F32) + zr[n, 3, 1].astype(F32)
        spot, slot = iota((NB * PACK, 2 * NB), 0), iota((NB * PACK, 2 * NB), 1)
        pick = onehot(spot == (slot // 2) * PACK + (slot % 2) * PIECES + n)
        term = mm(pick, total.astype(BF16))
        packf[...] = packf[...] + term if packed else term
        packed.append(n)

    def z_end():
        sent(zr.at[:, 0, :, pl.ds(0, NB), :], z_s.at[0])
        sent(zr.at[:, pl.ds(1, 3)], z_s.at[1])

    def decode():
        len_row, len_col, route_row, route_col, end_row, end_col, slot_row, slot_col = tables(
            lengths, route
        )
        n, patches = states.shape[0], lengths.shape[1]
        place = iota((n, patches), 0).astype(F32)
        member = onehot((place >= end_row - len_row) & (place < end_row))
        spot = iota((patches, NB * PACK), 1).astype(F32)
        target = route_col * PACK + slot_col * PIECES
        picks = jnp.concatenate([onehot(spot == target + j) for j in range(PIECES)], axis=0)
        values = mm(picks, arr2[...]).astype(BF16)
        total = jnp.zeros((patches, w_head.shape[1]), F32)
        for j in range(PIECES):
            total = total + mm(values[patches * j : patches * (j + 1), :], w_head[W * j : W * (j + 1), :])
        high = total.astype(BF16)
        low = (total - high.astype(F32)).astype(BF16)
        out[...] = (base[...] + mm(member, high) + mm(member, low)).astype(BF16)

    def own_logits():
        load_wait("head")
        base[...] = mm(states[...], w_head[...])

    def add_residual():
        load_wait("out")
        lw[...] = mm(lat[...], w_out[...])

    def exch():
        exchange_wait(snd, arr, a_s, a_r)
        slots()

    def ctx_go():
        ctx_send(0, 0)
        ctx_send(0, 1)

    def finish():
        sent(wsc.at[:, :, theirs], x_s.at[0])
        sent(wxo.at[:, half], x_s.at[1])
        relay_end()
        ctx_end()
        sums_end()
        z_end()

    stages = {
        START: start, RELAY: relay, PRODUCT: product, TURN: turn, SUM1: sum1,
        SUM2: sum2, GATHER1: gather1, GATHER2: gather2, GATHER3: gather3,
        JOINED: joined, EXCH: exch, CTXGO: ctx_go, RING: ctx_step, LAT: latents,
        RES: add_residual, MASK: mask, OWN: own_logits,
        PROJ: project, HEAD: head, ZF: z_first, ZA: z_add, ZL: z_last,
    }
    load_start()
    greet()
    load_wait("gain", "scale", "lengths", "route", "states")
    pool()
    load_wait("q", "k", "v", "ao")
    scale_weights()
    meet()
    swap_weights()
    start(0)
    start(1)
    exchange_start(snd, arr, a_s, a_r)
    for name, *where in ORDER:
        stages[name](*where)
    snd2[...] = packf[...].astype(BF16)
    exchange_start(snd2, arr2, b_s, b_r)
    exchange_wait(snd2, arr2, b_s, b_r)
    decode()
    finish()


def body(
    byte_states, enc_gain, patch_lengths, patch_route, w_in, latent_gain,
    w_query, w_key, w_value, w_attn_out, w_out, w_head,
):
    vmem = pl.BlockSpec(memory_space=pltpu.VMEM)
    far = pl.BlockSpec(memory_space=pl.ANY)
    dma = pltpu.SemaphoreType.DMA
    part_q, part_o = 3 * W // 16, W // 16

    def buf(*shape, dtype=BF16):
        return pltpu.VMEM(shape, dtype)

    inputs = (
        byte_states, enc_gain, patch_lengths, patch_route.reshape(1, -1), w_in,
        latent_gain.reshape(NB, -1), w_query, w_key, w_value, w_attn_out, w_out, w_head,
    )
    scratch = [
        *[buf(*value.shape, dtype=value.dtype) for value in inputs],
        dma((len(inputs),)),
        buf(STAGES, W, W),
        buf(3, 128, 2 * W),
        buf(3, W, W),
        buf(W, W),
        buf(PIECES, 3 * W, W),
        buf(PIECES, W, W),
        buf(PIECES, 2, 2 * part_q, W),
        buf(PIECES, 2, 4 * part_q, W),
        buf(PIECES, 3, 4 * part_o, W),
        buf(PIECES, 4 * part_q, W),
        buf(PIECES, 4 * part_o, W),
        buf(PIECES, 3, part_q, W),
        buf(PIECES, 3, part_o, W),
        buf(PIECES, 2, 3 * W, W),
        buf(PIECES, 2, W, W),
        buf(NB * PACK, W),
        buf(NB * PACK, W),
        buf(NB * PACK, W),
        buf(NB * PACK, W),
        buf(CTX, E + FLAGS),
        buf(CTX, 2 * W),
        buf(NT, 8, CTX, dtype=F32),
        buf(3, CTX, 2 * W, dtype=F32),
        buf(2, CTX, 2 * W),
        buf(CTX, 4 * W),
        buf(CTX, CTX, dtype=F32),
        buf(byte_states.shape[0], w_head.shape[1], dtype=F32),
        buf(4 * NB, 2 * W),
        buf(CTX, E, dtype=F32),
        buf(PIECES, CTX, W),
        buf(PIECES, 4, 2, 2 * NB, W),
        buf(NB * PACK, W, dtype=F32),
        dma((2,)), dma((STAGES, 2)), dma, dma((STAGES,)), dma((STAGES,)),
        dma((2,)), dma((2,)), dma, dma, dma((2,)), dma((2, 4, 2)), dma, dma,
        dma((7, 2)),
        dma((STAGES,)), dma((PIECES,)), dma((STAGES,)), dma((STAGES,)), dma((STAGES,)),
        dma((PIECES,)), dma((STAGES,)),
        dma((2,)), dma((PIECES, 4)), dma, dma,
    ]
    return pl.pallas_call(
        kernel,
        out_shape=jax.ShapeDtypeStruct((byte_states.shape[0], w_head.shape[1]), BF16),
        in_specs=[far] * 12,
        out_specs=vmem,
        scratch_shapes=scratch,
        compiler_params=pltpu.CompilerParams(
            collective_id=0, has_side_effects=True, vmem_limit_bytes=56 * 1024 * 1024
        ),
    )(
        *inputs
    )


def solution(mesh):
    return jax.shard_map(
        body,
        mesh=mesh,
        in_specs=(
            P(("byte", "tensor"), None),
            P(),
            P(("byte", "tensor"), None),
            P(("byte", "tensor"), None, None),
            P(None, "tensor"),
            P(),
            P("byte", "tensor"),
            P("byte", "tensor"),
            P("byte", "tensor"),
            P("tensor", "byte"),
            P("tensor", None),
            P(),
        ),
        out_specs=P(("byte", "tensor"), None),
        check_vma=False,
    )
```

```python
import jax
import jax.numpy as jnp
from jax import lax
from jax.experimental import pallas as pl
from jax.experimental.pallas import tpu as pltpu
from jax.sharding import PartitionSpec as P

MESH = pl.DeviceIdType.MESH
BF16 = jnp.bfloat16
F32 = jnp.float32
DH = 128
EPS = 1e-06
LANES = 128
EARLY, LATE = 8, 2
LOG2E = 1.4426950408889634
SIDE = 4
NB = 32
NT = 8
E = 1280
D = 4096
CTX = 512
W = 256
PIECES = E // W
STAGES = 2 * PIECES
FLAGS = 128
PACK = 16

(
    START, RELAY, PRODUCT, TURN, SUM1, SUM2, GATHER1, GATHER2, GATHER3, JOINED, EXCH,
    CTXGO, RING, LAT, MASK, OWN, PROJ, HEAD, ZF, ZA, ZL,
) = range(21)
ORDER = (
    (START, 2), (START, 3), (START, 4), (RELAY, 0, 1), (RELAY, 1, 1), (RELAY, 0, 2), (RELAY, 2, 1),
    (RELAY, 1, 2), (EXCH,), (RELAY, 3, 1), (RELAY, 0, 3), (START, 5), (RELAY, 2, 2), (RELAY, 4, 1),
    (RELAY, 1, 3), (START, 6), (RELAY, 3, 2), (RELAY, 0, 4), (RELAY, 5, 1), (RELAY, 2, 3),
    (START, 7), (RELAY, 4, 2), (PRODUCT, 0), (RELAY, 1, 4), (RELAY, 6, 1), (RELAY, 3, 3),
    (START, 8), (PRODUCT, 1), (RELAY, 5, 2), (RELAY, 2, 4), (RELAY, 7, 1), (RELAY, 4, 3),
    (PRODUCT, 2), (START, 9), (RELAY, 6, 2), (RELAY, 3, 4), (TURN, 0), (RELAY, 8, 1), (RELAY, 5, 3),
    (PRODUCT, 3), (RELAY, 7, 2), (RELAY, 4, 4), (TURN, 1), (RELAY, 9, 1), (RELAY, 6, 3),
    (PRODUCT, 4), (RELAY, 8, 2), (RELAY, 5, 4), (TURN, 2), (RELAY, 7, 3), (RELAY, 9, 2), (TURN, 3),
    (RELAY, 6, 4), (PRODUCT, 5), (SUM1, 0), (RELAY, 8, 3), (RELAY, 7, 4), (TURN, 4), (PRODUCT, 6),
    (SUM1, 1), (RELAY, 9, 3), (CTXGO,), (RELAY, 8, 4), (PRODUCT, 7), (SUM1, 2), (SUM1, 3),
    (RELAY, 9, 4), (PRODUCT, 8), (SUM1, 5), (RING, 0, 0), (SUM1, 4), (PRODUCT, 9), (SUM2, 0),
    (SUM1, 6), (RING, 0, 1), (SUM1, 7), (SUM2, 1), (SUM2, 2), (SUM2, 3), (RING, 1, 0), (SUM2, 4),
    (SUM1, 8), (SUM2, 5), (SUM2, 7), (RING, 1, 1), (SUM1, 9), (GATHER1, 1), (GATHER1, 0), (SUM2, 6),
    (GATHER1, 3), (GATHER1, 2), (GATHER1, 5), (RING, 2, 0), (GATHER1, 7), (GATHER1, 4), (SUM2, 8),
    (SUM2, 9), (RING, 2, 1), (GATHER2, 1), (RING, 3, 0), (GATHER2, 0), (GATHER1, 6), (RING, 3, 1),
    (GATHER2, 2), (GATHER2, 3), (MASK,), (LAT,), (GATHER3, 5), (GATHER2, 4), (GATHER1, 9),
    (GATHER3, 7), (GATHER3, 0), (GATHER1, 8), (GATHER3, 1), (JOINED, 5), (JOINED, 7), (GATHER3, 3),
    (GATHER3, 6), (JOINED, 0), (GATHER3, 2), (JOINED, 1), (GATHER3, 4), (GATHER3, 9), (JOINED, 3),
    (JOINED, 6), (JOINED, 2), (GATHER3, 8), (JOINED, 4), (JOINED, 9), (PROJ,), (HEAD, 0),
    (JOINED, 8), (ZF, 0), (ZF, 1), (ZF, 2), (ZF, 3), (ZF, 4), (HEAD, 1), (OWN,), (ZA, 0, 1),
    (ZA, 1, 1), (ZA, 2, 1), (ZA, 3, 1), (ZA, 4, 1), (HEAD, 2), (ZA, 0, 2), (ZA, 1, 2), (ZA, 2, 2),
    (ZA, 3, 2), (ZA, 4, 2), (HEAD, 3), (ZA, 0, 3), (ZA, 1, 3), (ZA, 2, 3), (ZA, 3, 3), (ZA, 4, 3),
    (HEAD, 4), (ZL, 0), (ZL, 1), (ZL, 2), (ZL, 3), (ZL, 4),
)


def mm(a, b):
    return jnp.dot(a, b, preferred_element_type=F32)


def mm_t(a, b):
    return lax.dot_general(a, b, (((1,), (1,)), ((), ())), preferred_element_type=F32)


def iota(shape, dim):
    return lax.broadcasted_iota(jnp.int32, shape, dim)


def onehot(mask):
    return jnp.where(mask, 1.0, 0.0).astype(BF16)


def tables(lengths, route):
    n = lengths.shape[1]
    down, across = iota((n, n), 0), iota((n, n), 1)
    eye = down == across

    def column(row):
        return jnp.sum(jnp.where(eye, row, 0.0), axis=1, keepdims=True)

    len_row = lengths[...].astype(F32)
    route_row = route[...].astype(F32)
    len_col, route_col = column(len_row), column(route_row)
    end_row = jnp.sum(jnp.where(down <= across, len_col, 0.0), axis=0, keepdims=True)
    end_col = jnp.sum(jnp.where(across <= down, len_row, 0.0), axis=1, keepdims=True)
    same = jnp.where(route_row == route_col, 1.0, 0.0)
    slot_row = jnp.sum(jnp.where(down < across, same, 0.0), axis=0, keepdims=True)
    slot_col = jnp.sum(jnp.where(across < down, same, 0.0), axis=1, keepdims=True)
    return len_row, len_col, route_row, route_col, end_row, end_col, slot_row, slot_col


def kernel(
    states_far, gain_far, lengths_far, route_far, w_in_far, lat_gain_far,
    w_q_far, w_k_far, w_v_far, w_ao_far, w_out_far, w_head_far, out,
    states, gain, lengths, route, w_in, lat_gain, w_q, w_k, w_v, w_ao, w_out, w_head, in_s,
    blk, wsc, wx, wxo, p_q, p_o, a1_q, b1_q, r1_o, t_q, t_o, r2_q, r2_o, m_q, m_o,
    snd, arr, snd2, arr2, ctx, lat, sqs, acc, qk, vals, bias, base, att, zp, zr, packf,
    w_s, w_r, p_s, p_r, loc, x_s, x_r, a_s, a_r, c_s, c_r, q_s, q_r,
    sum_s, a1_r, b1_r, r2_r, g1_r, g2_r, g3_r, h_r, z_s, z_r, b_s, b_r,
):
    b = lax.axis_index("byte")
    t = lax.axis_index("tensor")
    k = b % 2
    chip = b // 2
    x = chip % SIDE
    y = chip // SIDE
    far = (t - chip // 2 + NT) % NT
    up = (b, (t + 1) % NT)
    down = (b, (t + NT - 1) % NT)
    partner = (b + 1 - 2 * k, t)

    def rcopy(src, dst, ssem, rsem, dev):
        return pltpu.make_async_remote_copy(
            src_ref=src, dst_ref=dst, send_sem=ssem, recv_sem=rsem, device_id=dev, device_id_type=MESH
        )

    def send(src, dst, ssem, rsem, dev):
        rcopy(src, dst, ssem, rsem, dev).start()

    def got(dst, rsem):
        rcopy(dst, dst, rsem, rsem, partner).wait_recv()

    def sent(src, ssem):
        rcopy(src, src, ssem, ssem, partner).wait_send()

    def rows(start, size, step=16):
        return pl.ds(pl.multiple_of(start, step), size)

    bar = pltpu.get_barrier_semaphore()
    half = rows(128 * k, 128, 128)
    mine = rows(W * k, W, W)
    theirs = rows(W * (1 - k), W, W)

    def greet():
        @pl.loop(1, NB)
        def _(i):
            pl.semaphore_signal(bar, inc=1, device_id=((b + i) % NB, t), device_id_type=MESH)

        @pl.loop(1, NT)
        def _(i):
            pl.semaphore_signal(bar, inc=1, device_id=(b, (t + i) % NT), device_id_type=MESH)

    def scale_weights():
        g_row = lat_gain[pl.ds(b, 1), :]
        eye = iota((128, 128), 0) == iota((128, 128), 1)
        g_col = jnp.sum(jnp.where(eye, g_row, 0.0), axis=1, keepdims=True)
        for m, weight in enumerate((w_q, w_k, w_v)):
            wsc[m] = (weight[...].astype(F32) * g_col).astype(BF16)

    loads = {
        "gain": (lat_gain_far, lat_gain), "scale": (gain_far, gain), "lengths": (lengths_far, lengths),
        "route": (route_far, route), "states": (states_far, states), "q": (w_q_far, w_q),
        "k": (w_k_far, w_k), "v": (w_v_far, w_v), "ao": (w_ao_far, w_ao), "in": (w_in_far, w_in),
        "out": (w_out_far, w_out), "head": (w_head_far, w_head),
    }
    places = {name: i for i, name in enumerate(loads)}

    def load_start():
        for name, (src, dst) in loads.items():
            pltpu.make_async_copy(src, dst, in_s.at[places[name]]).start()

    def load_wait(*names):
        for name in names:
            src, dst = loads[name]
            pltpu.make_async_copy(src, dst, in_s.at[places[name]]).wait()

    def meet():
        pl.semaphore_wait(bar, NB + NT - 2)

    def swap_weights():
        for m in range(3):
            send(wsc.at[m, :, theirs], wx.at[m, half, :], x_s.at[0], x_r.at[0], partner)
        send(w_ao.at[theirs, :], wxo.at[:, half], x_s.at[1], x_r.at[1], partner)

    off = rows(W * (chip % 2), W, W)

    def cuts(j):
        return [rows(128 * k + 64 * i, 64, 64) for i in range(2)]

    def start(j):
        if j < PIECES:
            whole = w_in_far.at[pl.ds(W * j, W), off]
        else:
            whole = w_out_far.at[off, pl.ds(W * (j - PIECES), W)]

        @pl.when(far == 0)
        def _():
            for i, cut in enumerate(cuts(j)):
                if j < PIECES:
                    source = w_in_far.at[rows(W * j + 128 * k + 64 * i, 64, 64), off]
                else:
                    cols = pl.ds(W * (j - PIECES), W)
                    source = w_out_far.at[rows(W * (chip % 2) + 128 * k + 64 * i, 64, 64), cols]
                send(source, blk.at[j, cut, :], w_s.at[0], w_r.at[j, i], up)
                send(source, blk.at[j, cut, :], w_s.at[1], w_r.at[j, i], down)
            pltpu.make_async_copy(whole, blk.at[j], loc.at[j]).start()

    def relay(j, hops):
        last = NT // 2

        @pl.when(far == hops)
        def _():
            for i, cut in enumerate(cuts(j)):
                piece = blk.at[j, cut, :]
                got(piece, w_r.at[j, i])
                if hops < last:
                    send(piece, piece, w_s.at[0], w_r.at[j, i], up)
                send(piece, piece, p_s, p_r.at[j], partner)

        if hops < last:

            @pl.when(far == NT - hops)
            def _():
                for i, cut in enumerate(cuts(j)):
                    piece = blk.at[j, cut, :]
                    got(piece, w_r.at[j, i])
                    if hops < last - 1:
                        send(piece, piece, w_s.at[1], w_r.at[j, i], down)
                    send(piece, piece, p_s, p_r.at[j], partner)

    def relay_end():
        pieces = blk.at[:, half, :]

        @pl.when(far <= 3)
        def _():
            sent(pieces, w_s.at[0])

        @pl.when((far == 0) | (far >= 6))
        def _():
            sent(pieces, w_s.at[1])

        @pl.when(far != 0)
        def _():
            sent(pieces, p_s)

    def layout(j):
        if j < PIECES:
            return j, 3 * W // 16, (p_q, t_q, r2_q, m_q), 0
        return j - PIECES, W // 16, (p_o, t_o, r2_o, m_o), 1

    def axes(j):
        return (x, y) if j % 2 == 0 else (y, x)

    def peer(j, first, i):
        along_x = (j % 2 == 0) == first
        px = (x + i) % SIDE if along_x else x
        py = y if along_x else (y + i) % SIDE
        return ((py * SIDE + px) * 2 + k, t)

    def product(j):
        other = rows(128 * (1 - k), 128, 128)

        @pl.when(far == 0)
        def _():
            pltpu.make_async_copy(blk.at[j], blk.at[j], loc.at[j]).wait()

        @pl.when(far != 0)
        def _():
            got(blk.at[j, other, :], p_r.at[j])

        if j == 0:
            got(wx.at[:, other, :], x_r.at[0])
            for m in range(3):
                wx[m, half, :] = wsc[m, :, mine]
        if j == PIECES:
            got(wxo.at[:, other], x_r.at[1])
            wxo[:, half] = w_ao[mine, :]
        n, part, (p, tt, r2, m_), kind = layout(j)
        if j < PIECES:
            for m in range(3):
                p[n, W * m : W * (m + 1), :] = mm(blk[j], wx[m]).astype(BF16)
        else:
            p[n] = mm(wxo[...], blk[j]).astype(BF16)
        u, v = axes(j)
        if kind:
            for i in range(1, SIDE):
                block = rows(4 * part * ((u + i) % SIDE), 4 * part)
                send(
                    p.at[n, block, :], r1_o.at[n, i - 1],
                    sum_s.at[0, kind], a1_r.at[j], peer(j, True, i),
                )
            return
        for side, way in ((0, 1), (1, SIDE - 1)):
            block = rows(4 * part * ((u + 2) % SIDE) + 2 * part * side, 2 * part)
            send(
                p.at[n, block, :], a1_q.at[n, side],
                sum_s.at[0, kind], a1_r.at[j], peer(j, True, way),
            )

    def turn(j):
        n, part, (p, tt, r2, m_), kind = layout(j)
        u, v = axes(j)
        got(a1_q.at[n], a1_r.at[j])
        for side, way in ((0, 1), (1, SIDE - 1)):
            base = 4 * part * ((u + way) % SIDE)
            cut = rows(base + 2 * part * side, 2 * part)
            p[n, cut, :] = (p[n, cut, :].astype(F32) + a1_q[n, side].astype(F32)).astype(BF16)
            send(
                p.at[n, rows(base, 4 * part), :], b1_q.at[n, side],
                sum_s.at[1, kind], b1_r.at[j], peer(j, True, way),
            )

    def sum1(j):
        n, part, (p, tt, r2, m_), kind = layout(j)
        u, v = axes(j)
        total = p[n, rows(4 * part * u, 4 * part), :].astype(F32)
        if kind:
            got(r1_o.at[n], a1_r.at[j])
            total = total + r1_o[n, 0].astype(F32) + r1_o[n, 1].astype(F32) + r1_o[n, 2].astype(F32)
        else:
            got(b1_q.at[n], b1_r.at[j])
            total = total + b1_q[n, 0].astype(F32) + b1_q[n, 1].astype(F32)
        tt[n] = total.astype(BF16)
        for i in range(1, SIDE):
            to = (v + i) % SIDE
            send(
                tt.at[n, rows(part * to, part), :], r2.at[n, i - 1],
                sum_s.at[2, kind], r2_r.at[j], peer(j, False, i),
            )

    def sum2(j):
        n, part, (p, tt, r2, m_), kind = layout(j)
        u, v = axes(j)
        got(r2.at[n], r2_r.at[j])
        total = tt[n, rows(part * v, part), :].astype(F32)
        for i in range(SIDE - 1):
            total = total + r2[n, i].astype(F32)
        own = rows(part * (4 * u + v), part)
        m_[n, k, own, :] = total.astype(BF16)
        for i in range(1, SIDE):
            send(
                m_.at[n, k, own, :], m_.at[n, k, own, :],
                sum_s.at[3, kind], g1_r.at[j], peer(j, False, i),
            )

    def gather1(j):
        n, part, (p, tt, r2, m_), kind = layout(j)
        u, v = axes(j)
        got(r2.at[n], g1_r.at[j])
        own = rows(4 * part * u, 4 * part)
        for way in range(1, SIDE) if kind else (1, SIDE - 1):
            send(
                m_.at[n, k, own, :], m_.at[n, k, own, :],
                sum_s.at[4, kind], g2_r.at[j], peer(j, True, way),
            )

    def gather2(j):
        n, part, (p, tt, r2, m_), kind = layout(j)
        u, v = axes(j)
        got(b1_q.at[n], g2_r.at[j])
        for side, way in ((0, 1), (1, SIDE - 1)):
            base = 4 * part * ((u + SIDE - way) % SIDE) + 2 * part * side
            block = m_.at[n, k, rows(base, 2 * part), :]
            send(block, block, sum_s.at[5, kind], g3_r.at[j], peer(j, True, way))

    def gather3(j):
        n, part, (p, tt, r2, m_), kind = layout(j)
        if kind:
            got(r1_o.at[n], g2_r.at[j])
        else:
            got(a1_q.at[n], g3_r.at[j])
        send(m_.at[n, k], m_.at[n, k], sum_s.at[6, kind], h_r.at[j], partner)

    begun = []

    def joined(j):
        n, part, (p, tt, r2, m_), kind = layout(j)
        got(m_.at[n, 1 - k], h_r.at[j])
        if j < PIECES:
            piece = ctx[:, W * j : W * (j + 1)]
            for m in range(3):
                for side in range(2):
                    cols = slice(W * side, W * (side + 1))
                    term = mm(piece, m_[n, side, W * m : W * (m + 1), :])
                    if not begun:
                        acc[m, :, cols] = term
                    else:
                        acc[m, :, cols] = acc[m, :, cols] + term
            begun.append(j)

    def sums_end():
        for i, ref in enumerate((a1_q, b1_q, r2_q, r2_q, b1_q, a1_q, m_q.at[:, 0])):
            sent(ref, sum_s.at[i, 0])
        for i, ref in ((0, r1_o), (2, r2_o), (3, r2_o), (4, r1_o), (6, m_o.at[:, 0])):
            sent(ref, sum_s.at[i, 1])

    def pool():
        len_row, len_col, route_row, route_col, end_row, end_col, slot_row, slot_col = tables(
            lengths, route
        )
        values = states[...].astype(F32)
        scale = lax.rsqrt(jnp.mean(values * values, axis=-1, keepdims=True) + EPS)
        normed = values * scale * gain[...].reshape(1, -1)
        high = normed.astype(BF16)
        low = (normed - high.astype(F32)).astype(BF16)
        n = states.shape[0]
        place = iota((lengths.shape[1], n), 1).astype(F32)
        member = onehot((place >= end_col - len_col) & (place < end_col))
        pooled = ((mm(member, high) + mm(member, low)) / len_col).astype(BF16)
        spot = iota((NB * PACK, lengths.shape[1]), 0).astype(F32)
        target = route_row * PACK + slot_row * PIECES
        packed = mm(
            onehot(spot == route_row * PACK + 2 * PIECES + slot_row),
            jnp.ones((lengths.shape[1], W), BF16),
        )
        for j in range(PIECES):
            packed = packed + mm(onehot(spot == target + j), pooled[:, W * j : W * (j + 1)])
        snd[...] = packed.astype(BF16)

    def exchange_start(src, dst, ssem, rsem):
        own = rows(PACK * b, PACK)

        @pl.loop(1, NB)
        def _(i):
            to = (b + i) % NB
            send(src.at[rows(PACK * to, PACK), :], dst.at[own, :], ssem, rsem, (to, t))

        dst[own, :] = src[own, :]

    def exchange_wait(src, dst, ssem, rsem):
        most = pl.ds(0, (NB - 1) * PACK)
        sent(src.at[most, :], ssem)
        got(dst.at[most, :], rsem)

    def slots():
        slot, spot = iota((2 * NB, NB * PACK), 0), iota((2 * NB, NB * PACK), 1)
        base = (slot // 2) * PACK
        arrived = arr[...]
        own = rows(2 * NB * t, 2 * NB)
        for j in range(PIECES):
            pick = onehot(spot == base + (slot % 2) * PIECES + j)
            ctx[own, W * j : W * (j + 1)] = mm(pick, arrived).astype(BF16)
        pick = onehot(spot == base + 2 * PIECES + slot % 2)
        ctx[own, E : E + FLAGS] = mm(pick, arrived[:, :FLAGS]).astype(BF16)

    def ctx_cut(plane, cut):
        plane = (plane + 2 * NT) % NT
        return ctx.at[rows(2 * NB * plane + NB * cut, NB), :]

    def ctx_send(step, cut):
        for side, sign, dev in ((0, -1, up), (1, 1, down)):
            if step < 3 or side == cut:
                block = ctx_cut(t + sign * step, cut)
                send(block, block, c_s.at[side], c_r.at[side, step, cut], dev)

    def ctx_step(step, cut):
        for side, sign in ((0, -1), (1, 1)):
            if step < 3 or side == cut:
                got(ctx_cut(t + sign * (step + 1), cut), c_r.at[side, step, cut])
        if step < 3:
            ctx_send(step + 1, cut)

    def ctx_end():
        for side in range(2):
            sent(ctx.at[pl.ds(0, 7 * NB), :], c_s.at[side])

    def latents():
        load_wait("in", "out")
        part = mm(ctx[:, :E], w_in[...]).astype(BF16)
        lat[...] = part
        wide = part.astype(F32)
        squares = wide * wide
        high = squares.astype(BF16)
        low = (squares - high.astype(F32)).astype(BF16)
        ones = jnp.ones((8, part.shape[1]), BF16)
        sqs[t] = mm_t(ones, high) + mm_t(ones, low)

        @pl.loop(1, NT)
        def _(i):
            send(sqs.at[t], sqs.at[t], q_s, q_r, (b, (t + i) % NT))

    def scales():
        most = sqs.at[pl.ds(0, NT - 1)]
        sent(most, q_s)
        got(most, q_r)
        total = sqs[0]
        for i in range(1, NT):
            total = total + sqs[i]
        scale = lax.rsqrt(total / D + EPS)
        return jnp.transpose(scale)[:, 0:1]

    def project():
        scale = scales()
        for m in range(2):
            qk[m] = (acc[m] * scale).astype(BF16)
        values = (acc[2] * scale).astype(BF16)
        for h in range(values.shape[1] // DH):
            vals[:, 2 * DH * h : 2 * DH * h + DH] = values[:, DH * h : DH * (h + 1)]

    def mask():
        for h in range(vals.shape[1] // (2 * DH)):
            vals[:, 2 * DH * h + DH : 2 * DH * (h + 1)] = jnp.ones((CTX, DH), BF16)
        seen = mm_t(jnp.ones((8, FLAGS), BF16), ctx[:, E : E + FLAGS])[0:1, :] > 0.5
        line, place = iota((CTX, CTX), 0), iota((CTX, CTX), 1)
        allowed = ((place < line) & seen) | (place == line)
        bias[...] = jnp.where(allowed, 0.0, -1e30)

    def planes(step):
        return (t + 4,) if step == 0 else (t,) if step == 4 else (t + 4 - step, t - 4 + step)

    def head(step):
        lines = [z_rows(plane, 0, 2 * NB) for plane in planes(step)]
        size = 2 * NB * len(lines)
        asks = jnp.concatenate([qk[0, line, :] for line in lines], axis=0)
        hide = jnp.concatenate([bias[line, :] for line in lines], axis=0)
        for h in range(asks.shape[1] // DH):
            cols = slice(DH * h, DH * (h + 1))
            scores = mm_t(asks[:, cols], qk[1, :, cols]) * (DH ** (-0.5) * LOG2E) + hide
            raised = jnp.exp2(scores - jnp.max(scores, axis=-1, keepdims=True)).astype(BF16)
            mixed = mm(raised, vals[:, 2 * DH * h : 2 * DH * (h + 1)])
            att[0:size, cols] = (mixed[:, :DH] / mixed[:, DH:]).astype(BF16)

    def outputs(n, step):
        lines = [z_rows(plane, 0, 2 * NB) for plane in planes(step)]
        size = 2 * NB * len(lines)
        value = mm(att[0:size, :W], m_o[n, 0]) + mm(att[0:size, W:], m_o[n, 1])
        cols = slice(W * n, W * (n + 1))
        value = value + mm(jnp.concatenate([lat[line, :] for line in lines], axis=0), w_out[:, cols])
        return [value[2 * NB * i : 2 * NB * (i + 1), :] for i in range(len(lines))]

    def z_rows(plane, start, size):
        plane = (plane + 2 * NT) % NT
        return rows(2 * NB * plane + start, size)

    def z_first(n):
        zp[n, z_rows(t + 4, 0, 2 * NB), :] = outputs(n, 0)[0].astype(BF16)
        for side, dev in ((0, up), (1, down)):
            send(
                zp.at[n, z_rows(t + 4, NB * side, NB), :], zr.at[n, 0, side, pl.ds(0, NB), :],
                z_s.at[0], z_r.at[n, 0], dev,
            )

    def z_add(n, step):
        values = outputs(n, step)
        if step == 1:
            got(zr.at[n, 0, :, pl.ds(0, NB), :], z_r.at[n, 0])
        else:
            got(zr.at[n, step - 1], z_r.at[n, step - 1])
        for side, sign, dev in ((0, 1, up), (1, -1, down)):
            value = values[side]
            place = z_rows(t + sign * (4 - step), 0, 2 * NB)
            if step == 1:
                came = zr[n, 0, side, 0:NB, :].astype(F32)
                whole = [value[:NB, :], value[NB:, :]]
                whole[side] = whole[side] + came
                value = jnp.concatenate(whole, axis=0)
            else:
                value = value + zr[n, step - 1, side].astype(F32)
            zp[n, place, :] = value.astype(BF16)
            send(zp.at[n, place, :], zr.at[n, step, side], z_s.at[1], z_r.at[n, step], dev)

    packed = []

    def z_last(n):
        total = outputs(n, 4)[0]
        got(zr.at[n, 3], z_r.at[n, 3])
        total = total + zr[n, 3, 0].astype(F32) + zr[n, 3, 1].astype(F32)
        value = total.astype(BF16)
        spot, slot = iota((NB * PACK, 2 * NB), 0), iota((NB * PACK, 2 * NB), 1)
        early = n < PIECES - 1
        base_row = (slot // 2) * PACK + (slot % 2) * (EARLY if early else LATE) + (2 * n if early else 0)
        term = mm(onehot(spot == base_row), value[:, :LANES])
        term = term + mm(onehot(spot == base_row + 1), value[:, LANES:])
        if not early:
            snd2[1] = term.astype(BF16)
            exchange_start(snd2.at[1], arr2.at[1], b_s.at[1], b_r.at[1])
            return
        packf[...] = packf[...] + term if packed else term
        packed.append(n)
        if len(packed) == PIECES - 1:
            snd2[0] = packf[...].astype(BF16)
            exchange_start(snd2.at[0], arr2.at[0], b_s.at[0], b_r.at[0])

    def z_end():
        sent(zr.at[:, 0, :, pl.ds(0, NB), :], z_s.at[0])
        sent(zr.at[:, pl.ds(1, 3)], z_s.at[1])

    def decode():
        len_row, len_col, route_row, route_col, end_row, end_col, slot_row, slot_col = tables(
            lengths, route
        )
        n, patches = states.shape[0], lengths.shape[1]
        place = iota((n, patches), 0).astype(F32)
        member = onehot((place >= end_row - len_row) & (place < end_row))
        spot = iota((patches, NB * PACK), 1).astype(F32)
        total = jnp.zeros((patches, w_head.shape[1]), F32)
        for group, count in enumerate((EARLY, LATE)):
            target = route_col * PACK + slot_col * count
            picks = jnp.concatenate([onehot(spot == target + j) for j in range(count)], axis=0)
            exchange_wait(snd2.at[group], arr2.at[group], b_s.at[group], b_r.at[group])
            values = mm(picks, arr2[group]).astype(BF16)
            for j in range(count):
                line = LANES * (EARLY * group + j)
                total = total + mm(
                    values[patches * j : patches * (j + 1), :], w_head[line : line + LANES, :]
                )
        high = total.astype(BF16)
        low = (total - high.astype(F32)).astype(BF16)
        out[...] = (base[...] + mm(member, high) + mm(member, low)).astype(BF16)

    def own_logits():
        load_wait("head")
        base[...] = mm(states[...], w_head[...])

    def exch():
        exchange_wait(snd, arr, a_s, a_r)
        slots()

    def ctx_go():
        ctx_send(0, 0)
        ctx_send(0, 1)

    def finish():
        sent(wsc.at[:, :, theirs], x_s.at[0])
        sent(wxo.at[:, half], x_s.at[1])
        relay_end()
        ctx_end()
        sums_end()
        z_end()

    stages = {
        START: start, RELAY: relay, PRODUCT: product, TURN: turn, SUM1: sum1,
        SUM2: sum2, GATHER1: gather1, GATHER2: gather2, GATHER3: gather3,
        JOINED: joined, EXCH: exch, CTXGO: ctx_go, RING: ctx_step, LAT: latents,
        MASK: mask, OWN: own_logits,
        PROJ: project, HEAD: head, ZF: z_first, ZA: z_add, ZL: z_last,
    }
    load_start()
    greet()
    load_wait("gain", "scale", "lengths", "route", "states")
    pool()
    load_wait("q", "k", "v", "ao")
    scale_weights()
    meet()
    swap_weights()
    start(0)
    start(1)
    exchange_start(snd, arr, a_s, a_r)
    for name, *where in ORDER:
        stages[name](*where)
    decode()
    finish()


def body(
    byte_states, enc_gain, patch_lengths, patch_route, w_in, latent_gain,
    w_query, w_key, w_value, w_attn_out, w_out, w_head,
):
    vmem = pl.BlockSpec(memory_space=pltpu.VMEM)
    far = pl.BlockSpec(memory_space=pl.ANY)
    dma = pltpu.SemaphoreType.DMA
    part_q, part_o = 3 * W // 16, W // 16

    def buf(*shape, dtype=BF16):
        return pltpu.VMEM(shape, dtype)

    inputs = (
        byte_states, enc_gain, patch_lengths, patch_route.reshape(1, -1), w_in,
        latent_gain.reshape(NB, -1), w_query, w_key, w_value, w_attn_out, w_out, w_head,
    )
    scratch = [
        *[buf(*value.shape, dtype=value.dtype) for value in inputs],
        dma((len(inputs),)),
        buf(STAGES, W, W),
        buf(3, 128, 2 * W),
        buf(3, W, W),
        buf(W, W),
        buf(PIECES, 3 * W, W),
        buf(PIECES, W, W),
        buf(PIECES, 2, 2 * part_q, W),
        buf(PIECES, 2, 4 * part_q, W),
        buf(PIECES, 3, 4 * part_o, W),
        buf(PIECES, 4 * part_q, W),
        buf(PIECES, 4 * part_o, W),
        buf(PIECES, 3, part_q, W),
        buf(PIECES, 3, part_o, W),
        buf(PIECES, 2, 3 * W, W),
        buf(PIECES, 2, W, W),
        buf(NB * PACK, W),
        buf(NB * PACK, W),
        buf(2, NB * PACK, LANES),
        buf(2, NB * PACK, LANES),
        buf(CTX, E + FLAGS),
        buf(CTX, 2 * W),
        buf(NT, 8, CTX, dtype=F32),
        buf(3, CTX, 2 * W, dtype=F32),
        buf(2, CTX, 2 * W),
        buf(CTX, 4 * W),
        buf(CTX, CTX, dtype=F32),
        buf(byte_states.shape[0], w_head.shape[1], dtype=F32),
        buf(4 * NB, 2 * W),
        buf(PIECES, CTX, W),
        buf(PIECES, 4, 2, 2 * NB, W),
        buf(NB * PACK, LANES, dtype=F32),
        dma((2,)), dma((STAGES, 2)), dma, dma((STAGES,)), dma((STAGES,)),
        dma((2,)), dma((2,)), dma, dma, dma((2,)), dma((2, 4, 2)), dma, dma,
        dma((7, 2)),
        dma((STAGES,)), dma((PIECES,)), dma((STAGES,)), dma((STAGES,)), dma((STAGES,)),
        dma((PIECES,)), dma((STAGES,)),
        dma((2,)), dma((PIECES, 4)), dma((2,)), dma((2,)),
    ]
    return pl.pallas_call(
        kernel,
        out_shape=jax.ShapeDtypeStruct((byte_states.shape[0], w_head.shape[1]), BF16),
        in_specs=[far] * 12,
        out_specs=vmem,
        scratch_shapes=scratch,
        compiler_params=pltpu.CompilerParams(
            collective_id=0, has_side_effects=True, vmem_limit_bytes=56 * 1024 * 1024
        ),
    )(
        *inputs
    )


def solution(mesh):
    return jax.shard_map(
        body,
        mesh=mesh,
        in_specs=(
            P(("byte", "tensor"), None),
            P(),
            P(("byte", "tensor"), None),
            P(("byte", "tensor"), None, None),
            P(None, "tensor"),
            P(),
            P("byte", "tensor"),
            P("byte", "tensor"),
            P("byte", "tensor"),
            P("tensor", "byte"),
            P("tensor", None),
            P(),
        ),
        out_specs=P(("byte", "tensor"), None),
        check_vma=False,
    )
```
